32 devices in a mesh: scan: 4 (over y, x), slab: 8 (over z, core).
Axes of the slice: x: 2, y: 2, z: 4, core: 2. Of those that a mesh axis runs over, the one named last changes fastest.
Arguments:
- volume: float32 [4, 4096, 1024], P('scan', 'slab'), may hold values from -108 to 108
- velocity0: float32 [4, 4096], P('scan', 'slab'), may hold values from -0.5 to 0.5
- fetch_slab: int32 [4, 2, 4096, 1], P('scan', None, 'slab'), may hold values from 0 to 7; in each aligned block of 512 rows (0 to 511, 512 to 1023, ..., all dimensions but the last counted through in order) at most 96 rows name the same one
- fetch_row: int32 [4, 2, 4096], P('scan', None, 'slab'), may hold values from 0 to 511
- modulus_class: int32 [4, 4096], P('scan', 'slab'), may hold values from 0 to 3
- modulus_table: float32 [4], replicated, may hold values from 200 to 3000
Outputs:
- velocity: float32 [4, 4096], P('scan', 'slab')
- misfit: float32 [4, 4096, 1024], P('scan', 'slab')
The draws below stay inside these ranges and needn't reach their ends.
Inputs may be any that keep to these rules, and one draw needn't show every extreme that they name: `fetch_slab`: among the rows of one device for one direction, at most 96 name the same slab, a bound that some block reaches of them.
All inputs are finite; a program needn't handle non-finite values.
Results may differ from the reference program's by a relative error of at most 0.00011.
Values sent between devices are 32-bit elements; how exact they have to be, the bound alone decides.
No kernel may reach another device: no remote copies, remote signals or barrier semaphores. Data moves between devices by JAX's collectives and lax.ppermute only.
A program may use at most 64 MiB of HBM per device.

```python
import math
import jax
import jax.numpy as jnp
import numpy as np
from jax import lax

X = 1024
RD = 512
Y = 1024
BAND = 32
NCLASS = 4
ITERS = 2
SCANS = 4
ROWS = 4096
CAP = 96
N_SLAB = 8


def draw_volume(key, part):
    keys = jax.random.split(key, 3)
    shape = (SCANS, ROWS, X)
    base = jnp.clip(jax.random.normal(keys[0], shape, jnp.float32), -6.0, 6.0)
    contrast = jnp.exp(jax.random.uniform(keys[1], (SCANS, ROWS, 1), jnp.float32, math.log(0.3), math.log(3.0)))
    columns = jnp.exp(jax.random.uniform(keys[2], (1, 1, X), jnp.float32, math.log(0.5), math.log(2.0)))
    position = lax.broadcasted_iota(jnp.int32, (1, ROWS, 1), 1).astype(jnp.float32)
    ramp = 1.0 + 2.0 * position / float(max(ROWS - 1, 1))
    return base * contrast * columns * ramp


def set_ends(entries, own_key, least, top_value):
    index_at = [jax.random.randint(jax.random.fold_in(own_key, axis), (), 0, length) for axis, length in enumerate(entries.shape)]
    longest = entries.shape.index(max(entries.shape))
    neighbour = index_at[:longest] + [(index_at[longest] + 1) % entries.shape[longest]] + index_at[longest + 1:]
    return entries.at[tuple(index_at)].set(least).at[tuple(neighbour)].set(top_value)


def level_of(key, shape, cuts, low, high):
    gain = 1.0
    for axis_at, parts in cuts:
        heights = jax.random.uniform(jax.random.fold_in(jax.random.fold_in(key, 6), axis_at), (parts,), jnp.float32, low / len(cuts), high / len(cuts))
        gain = gain * jnp.repeat(jnp.exp(heights), shape[axis_at] // parts).reshape((-1,) + (1,) * (len(shape) - 1 - axis_at))
    return gain


def routed_block(own_key, own, number, rows, amount, top, bound, skew):
    ranking = jax.random.permutation(own_key, amount)
    packed, ordinary = portions_of(amount, rows * top, bound, skew, True), portions_of(amount, rows * top, bound, skew, False)
    places = jnp.arange(amount)

    def named(sizes, rotation):
        used = int((sizes > 0).sum())
        fixed = max(1, used // 4)
        passed = fixed + (places - fixed + rotation * (used - fixed)) % max(1, amount - fixed)
        return jnp.zeros((amount,), jnp.int32).at[ranking[jnp.where(places < fixed, places, passed)]].set(jnp.asarray(sizes, jnp.int32))

    sizes = jnp.where(number % 4 == 0, named(packed, number // 4), named(ordinary, number - number // 4 - 1))
    mixed = jax.random.permutation(jax.random.fold_in(own, 3), amount)
    source_of, sink = mixed[0:amount // 2 * 2:2], mixed[1:amount // 2 * 2:2]
    room = jnp.minimum(sizes[source_of] - 1, bound - sizes[sink]) // 2
    room = jnp.where((source_of == ranking[0]) | (sink == ranking[0]) | (sizes[sink] == 0), 0, jnp.maximum(room, 0))
    passed = jax.random.randint(jax.random.fold_in(own, 4), (amount // 2,), 0, 1 << 20) % (room + 1)
    sizes = sizes.at[source_of].add(-passed).at[sink].add(passed)
    labels = jnp.searchsorted(jnp.cumsum(sizes), jnp.arange(rows * top), side="right").astype(jnp.int32)
    table = labels.reshape(top, rows).T
    table = table[jax.random.permutation(jax.random.fold_in(own, 1), rows)]
    rotation = jax.random.randint(jax.random.fold_in(own, 2), (rows, 1), 0, top)
    return jnp.take_along_axis(table, (jnp.arange(top)[None, :] + rotation) % top, axis=1)


def portions_of(number_of, total, limit, lean, full):
    weights = [(1 << 20) // math.isqrt(grade ** lean) + 1 for grade in range(1, number_of + 1)]
    largest = limit if full else min(limit, max(-(-total // number_of), total * weights[0] // sum(weights)))
    least = 1 if total - largest >= number_of - 1 else 0
    holding, rest = [largest] + [least] * (number_of - 1), total - largest - least * (number_of - 1)
    while rest > 0:
        candidates = [i for i in range(1, number_of) if holding[i] < largest] or [i for i in range(1, number_of) if holding[i] < limit]
        mass, budget = sum([weights[i] for i in candidates]), rest
        for i in candidates:
            more = min(limit - holding[i], max(1, budget * weights[i] // mass), rest)
            holding[i] = holding[i] + more
            rest = rest - more
    return np.array(holding)


def setup_inputs(seed: int = 0) -> dict:
    key_list = jax.random.split(jax.random.key(seed), 7)
    volume = draw_volume(jax.random.fold_in(key_list[6], 71), 0)
    velocity0 = jnp.clip(jax.random.uniform(key_list[1], (SCANS, ROWS), jnp.float32, -0.5, 0.5) * level_of(key_list[1], (SCANS, ROWS), ((0, 4), (1, 8)), -0.4, 0.0), -0.5, 0.5)
    fetch_slab_keys = jax.random.split(jax.random.fold_in(key_list[2], 1), SCANS * 2 * ROWS // RD)
    fetch_slab_turns = jax.random.permutation(jax.random.fold_in(key_list[2], 3), SCANS * 2 * ROWS // RD)
    fetch_slab = jax.vmap(lambda own, number: routed_block(jax.random.fold_in(key_list[2], 2), own, number, RD, N_SLAB, 1, CAP, 2))(fetch_slab_keys, fetch_slab_turns).reshape((SCANS, 2, ROWS, 1))
    fetch_row = set_ends(jax.random.randint(key_list[3], (SCANS, 2, ROWS), 0, RD), jax.random.fold_in(key_list[3], 1), 0, RD - 1).astype(jnp.int32)
    modulus_class = set_ends(jax.random.randint(key_list[4], (SCANS, ROWS), 0, NCLASS), jax.random.fold_in(key_list[4], 1), 0, NCLASS - 1).astype(jnp.int32)
    modulus_table = jnp.clip(jnp.exp(jax.random.uniform(key_list[5], (NCLASS,), jnp.float32, math.log(200.0), math.log(3000.0))), 200.0, 3000.0)
    return {"volume": volume, "velocity0": velocity0, "fetch_slab": fetch_slab, "fetch_row": fetch_row, "modulus_class": modulus_class, "modulus_table": modulus_table}


root_three = math.sqrt(3.0)
pole_value = math.sqrt(3.0) - 2.0

def filter_block(block_width, band_reach):
    offsets = lax.broadcasted_iota(jnp.int32, (3 * block_width, block_width), 0) - block_width - lax.broadcasted_iota(jnp.int32, (3 * block_width, block_width), 1)
    distance = jnp.abs(offsets)
    parity = 1.0 - 2.0 * (distance % 2).astype(jnp.float32)
    magnitude = jnp.exp(distance.astype(jnp.float32) * math.log(-pole_value))
    return jnp.where(distance <= band_reach, root_three * parity * magnitude, jnp.zeros_like(magnitude))

def prefilter(voxels):
    length = voxels.shape[1]
    block_width = min(128, length)
    matrix = filter_block(block_width, BAND)
    padded = jnp.pad(voxels, ((0, 0), (block_width, block_width)))
    pieces = []
    for number in range(length // block_width):
        window = padded[:, number * block_width:number * block_width + 3 * block_width]
        pieces.append(jnp.dot(window, matrix, preferred_element_type=jnp.float32, precision=lax.Precision.HIGHEST))
    return jnp.concatenate(pieces, axis=1)

def taylor_terms(coeffs):
    padded = jnp.pad(coeffs, ((0, 0), (1, 1)))
    before = padded[:, :-2]
    after = padded[:, 2:]
    value = (before + 4.0 * coeffs + after) / 6.0
    slope = 0.5 * (after - before)
    bend = after - 2.0 * coeffs + before
    return (value, slope, bend)

def residuals(forward, backward, voxels, velocity):
    moved = velocity[:, None]
    fwd_value, fwd_slope, fwd_bend = taylor_terms(forward)
    bwd_value, bwd_slope, bwd_bend = taylor_terms(backward)
    res_fwd = fwd_value + moved * fwd_slope + 0.5 * moved * moved * fwd_bend - voxels
    jac_fwd = fwd_slope + moved * fwd_bend
    res_bwd = bwd_value - moved * bwd_slope + 0.5 * moved * moved * bwd_bend - voxels
    jac_bwd = moved * bwd_bend - bwd_slope
    return (res_fwd, jac_fwd, res_bwd, jac_bwd)

def row_terms(forward, backward, voxels, velocity):
    res_fwd, jac_fwd, res_bwd, jac_bwd = residuals(forward, backward, voxels, velocity)
    linear = lax.optimization_barrier(jnp.sum(jac_fwd * res_fwd + jac_bwd * res_bwd, axis=1))
    curvature = lax.optimization_barrier(jnp.sum(jac_fwd * jac_fwd + jac_bwd * jac_bwd, axis=1))
    return (linear, curvature)

def laplace(extended, margin, reach, length):
    centre = lax.slice_in_dim(extended, margin, margin + length)
    near = lax.slice_in_dim(extended, margin - 1, margin - 1 + length) + lax.slice_in_dim(extended, margin + 1, margin + 1 + length)
    far = lax.slice_in_dim(extended, margin - reach, margin - reach + length) + lax.slice_in_dim(extended, margin + reach, margin + reach + length)
    return 4.0 * centre - near - far

def stencil(field):
    length = field.shape[0]
    return laplace(jnp.pad(field, (Y, Y)), Y, Y, length)

def reference(volume, velocity0, fetch_slab, fetch_row, modulus_class, modulus_table):
    scans = volume.shape[0]
    coefficients = [prefilter(volume[number]) for number in range(scans)]
    forwards = []
    backwards = []
    for number in range(scans):
        index_fwd = (fetch_slab[number, 0, :, 0] * RD + fetch_row[number, 0]).astype(jnp.int32)
        index_bwd = (fetch_slab[number, 1, :, 0] * RD + fetch_row[number, 1]).astype(jnp.int32)
        if number + 1 < scans:
            forwards.append(jnp.take(coefficients[number + 1], index_fwd, axis=0))
        else:
            forwards.append(jnp.zeros_like(volume[number]))
        if number > 0:
            backwards.append(jnp.take(coefficients[number - 1], index_bwd, axis=0))
        else:
            backwards.append(jnp.zeros_like(volume[number]))
    coefficients = None
    classes = lax.broadcasted_iota(jnp.int32, (1, 1, modulus_table.shape[0]), 2)
    weight = lax.optimization_barrier(jnp.sum(jnp.where(modulus_class[:, :, None] == classes, modulus_table[None, None, :], jnp.zeros_like(modulus_table)[None, None, :]), axis=2))
    stiffness = jnp.sqrt(weight)
    velocity = velocity0
    for iteration in range(ITERS):
        linears = []
        curvatures = []
        for number in range(scans):
            linear, curvature = row_terms(forwards[number], backwards[number], volume[number], velocity[number])
            linears.append(linear)
            curvatures.append(curvature)
        linear = jnp.stack(linears)
        curvature = jnp.stack(curvatures)
        scaled = stiffness * velocity
        gradient = linear + stiffness * jnp.stack([stencil(scaled[number]) for number in range(scans)])
        diagonal = curvature + 4.0 * stiffness * stiffness
        direction = gradient / diagonal
        scaled_dir = stiffness * direction
        bend_term = scaled_dir * jnp.stack([stencil(scaled_dir[number]) for number in range(scans)])
        upper = jnp.sum(direction * gradient)
        lower = jnp.sum(curvature * direction * direction + bend_term)
        velocity = velocity - upper / lower * direction
    misfits = []
    for number in range(scans):
        res_fwd, jac_fwd, res_bwd, jac_bwd = residuals(forwards[number], backwards[number], volume[number], velocity[number])
        misfits.append(res_fwd + res_bwd)
    return (velocity, jnp.stack(misfits))
```

```python
import functools
import math

import jax
import jax.numpy as jnp
import numpy as np
from jax import lax
from jax.experimental import pallas as pl
from jax.experimental.pallas import tpu as pltpu
from jax.sharding import PartitionSpec as P

Y = 1024
BAND = 32
ITERS = 2
SUMS = 5
FIELDS = 7
VMEM = pl.BlockSpec(memory_space=pltpu.VMEM)
SMEM = pl.BlockSpec(memory_space=pltpu.SMEM)
LIMIT = pltpu.CompilerParams(vmem_limit_bytes=32 * 1024 * 1024)


def filter_parts(width, rim):
    offsets = np.arange(width + 2 * rim)[:, None] - rim - np.arange(width)[None, :]
    distance = np.abs(offsets)
    pole = math.sqrt(3.0) - 2.0
    exact = np.where(distance <= BAND, math.sqrt(3.0) * pole ** np.minimum(distance, BAND), 0.0)
    exact = exact.astype(np.float32)
    high = exact.astype(jnp.bfloat16)
    low = (exact - high.astype(np.float32)).astype(jnp.bfloat16)
    return high, low


def prefilter_kernel(width, rim, vol_ref, high_ref, low_ref, left_ref, right_ref):
    columns = vol_ref.shape[1]
    half = columns // 2
    voxels = vol_ref[...]
    high = voxels.astype(jnp.bfloat16)
    low = (voxels - high.astype(jnp.float32)).astype(jnp.bfloat16)
    for start in range(0, columns, width):
        first, last = max(0, start - rim), min(columns, start + width + rim)
        top = first - (start - rim)
        rows = slice(top, top + last - first)
        dot = functools.partial(jnp.dot, preferred_element_type=jnp.float32)
        out = dot(high[:, first:last], low_ref[rows, :]) + dot(low[:, first:last], high_ref[rows, :])
        out = out + dot(high[:, first:last], high_ref[rows, :])
        if start < half:
            left_ref[:, start : start + width] = out
        else:
            right_ref[:, start - half : start - half + width] = out


def prefilter(voxels):
    rows, columns = voxels.shape
    width, rim, block = 256, 128, 128
    high, low = filter_parts(width, rim)
    whole = pl.BlockSpec((width + 2 * rim, width), lambda i: (0, 0))
    halves = jax.ShapeDtypeStruct((rows, columns // 2), jnp.float32)
    return pl.pallas_call(
        functools.partial(prefilter_kernel, width, rim),
        grid=(rows // block,),
        in_specs=[pl.BlockSpec((block, columns), lambda i: (i, 0)), whole, whole],
        out_specs=[pl.BlockSpec((block, columns // 2), lambda i: (i, 0))] * 2,
        out_shape=[halves, halves],
        compiler_params=LIMIT,
        name="prefilter",
    )(voxels, jnp.asarray(high), jnp.asarray(low))


def request_kernel(devices, capacity, names_ref, table_ref, place_ref):
    sets, rows = names_ref.shape
    before = lax.broadcasted_iota(jnp.int32, (rows, rows), 0)
    after = lax.broadcasted_iota(jnp.int32, (rows, rows), 1)
    earlier = jnp.where(before < after, 1.0, 0.0).astype(jnp.bfloat16)
    peers = lax.broadcasted_iota(jnp.int32, (devices, rows), 0)
    slots = lax.broadcasted_iota(jnp.int32, (devices * capacity, rows), 0)
    digit = lax.broadcasted_iota(jnp.int32, (8, rows), 0)
    for number in range(sets):
        name = names_ref[number : number + 1, :]
        peer = name // rows
        row = name - peer * rows
        hit = jnp.where(peers == peer, 1.0, 0.0)
        running = jnp.dot(hit.astype(jnp.bfloat16), earlier, preferred_element_type=jnp.float32)
        slot = jnp.sum(hit * running, axis=0, keepdims=True).astype(jnp.int32)
        place = peer * capacity + slot
        place_ref[number : number + 1, :] = place
        taken = jnp.where(slots == place, 1.0, 0.0).astype(jnp.bfloat16)
        digits = jnp.where(digit == 0, row // 16, jnp.where(digit == 1, row % 16, 0))
        found = lax.dot_general(
            digits.astype(jnp.float32).astype(jnp.bfloat16),
            taken,
            (((1,), (1,)), ((), ())),
            preferred_element_type=jnp.float32,
        )
        table_ref[number : number + 1, :] = (16.0 * found[0:1] + found[1:2]).astype(jnp.int32)


def requests(names, devices, capacity):
    sets, rows = names.shape
    return pl.pallas_call(
        functools.partial(request_kernel, devices, capacity),
        in_specs=[VMEM],
        out_specs=[VMEM, VMEM],
        out_shape=[
            jax.ShapeDtypeStruct((sets, devices * capacity), jnp.int32),
            jax.ShapeDtypeStruct((sets, rows), jnp.int32),
        ],
        compiler_params=LIMIT,
        name="requests",
    )(names)


def taylor(coeffs):
    columns = coeffs.shape[1]
    column = lax.broadcasted_iota(jnp.int32, coeffs.shape, 1)
    before = jnp.where(column == 0, 0.0, pltpu.roll(coeffs, 1, 1))
    after = jnp.where(column == columns - 1, 0.0, pltpu.roll(coeffs, columns - 1, 1))
    bend = after - 2.0 * coeffs + before
    return (before + 4.0 * coeffs + after) * (1.0 / 6.0), 0.5 * (after - before), bend


def pair(left_ref, right_ref):
    return jnp.concatenate([left_ref[...], right_ref[...]], axis=1)


def lanes(values):
    rows, columns = values.shape
    total = values[:, 0:128]
    for start in range(128, columns, 128):
        total = total + values[:, start : start + 128]
    return jnp.sum(total.T, axis=0, keepdims=True)


def sums_kernel(sign_ref, near0, near1, far0, far1, vol_ref, out_ref):
    sign = sign_ref[0]
    voxels = vol_ref[...]
    value, slope, bend = taylor(pair(near0, near1))
    other_value, other_slope, other_bend = taylor(pair(far0, far1))
    value = value - voxels
    other_value = other_value - voxels
    slope = sign * slope
    other_slope = -sign * other_slope
    c0 = slope * slope + other_slope * other_slope
    out_ref[0:1, :] = lanes(slope * value + other_slope * other_value)
    out_ref[1:2, :] = lanes(c0 + bend * value + other_bend * other_value)
    out_ref[2:3, :] = lanes(c0)
    out_ref[3:4, :] = lanes(2.0 * (slope * bend + other_slope * other_bend))
    out_ref[4:5, :] = lanes(bend * bend + other_bend * other_bend)


def row_sums(sign, streams, voxels):
    rows, columns = voxels.shape
    block = 128
    half = pl.BlockSpec((block, columns // 2), lambda i: (i, 0))
    return pl.pallas_call(
        sums_kernel,
        grid=(rows // block,),
        in_specs=[SMEM, half, half, half, half, pl.BlockSpec((block, columns), lambda i: (i, 0))],
        out_specs=pl.BlockSpec((SUMS, block), lambda i: (0, i)),
        out_shape=jax.ShapeDtypeStruct((SUMS, rows), jnp.float32),
        compiler_params=LIMIT,
        name="row_sums",
    )(sign, *streams, voxels)


def plane_stencil(field, slabs):
    rows = field.shape[1]
    hops = Y // rows
    slab = lax.broadcasted_iota(jnp.int32, field.shape, 0) % slabs
    row = lax.broadcasted_iota(jnp.int32, field.shape, 1)

    def moved(cells, by):
        kept = slab >= by if by > 0 else slab < slabs + by
        return jnp.where(kept, pltpu.roll(cells, by % cells.shape[0], 0), 0.0)

    low = pltpu.roll(field, 1, 1)
    high = pltpu.roll(field, rows - 1, 1)
    low = jnp.where(row == 0, moved(low, 1), low)
    high = jnp.where(row == rows - 1, moved(high, -1), high)
    return 4.0 * field - low - high - moved(field, hops) - moved(field, -hops)


def final_kernel(slabs, where_ref, sign_ref, fields_ref, near0, near1, far0, far1, vol_ref, velocity_ref, misfit_ref, moved_ref):
    step = pl.program_id(0)
    rows = velocity_ref.shape[1]
    block = vol_ref.shape[0]

    @pl.when(step == 0)
    def _():
        l0, l1, c0, c1, c2, velocity, stiffness = [
            fields_ref[:, i * rows : (i + 1) * rows] for i in range(FIELDS)
        ]
        for _ in range(ITERS):
            linear = l0 + velocity * (l1 + velocity * (0.75 * c1 + velocity * (0.5 * c2)))
            curvature = c0 + velocity * (c1 + velocity * c2)
            gradient = linear + stiffness * plane_stencil(stiffness * velocity, slabs)
            direction = gradient / (curvature + 4.0 * stiffness * stiffness)
            scaled = stiffness * direction
            bent = curvature * direction * direction + scaled * plane_stencil(scaled, slabs)
            upper = jnp.sum(direction * gradient, keepdims=True)
            lower = jnp.sum(bent, keepdims=True)
            velocity = velocity - upper / lower * direction
        device = lax.broadcasted_iota(jnp.int32, velocity.shape, 0)
        own = jnp.sum(jnp.where(device == where_ref[0], velocity, 0.0), axis=0, keepdims=True)
        velocity_ref[...] = own
        for start in range(0, rows, 128):
            moved_ref[start : start + 128, :] = jnp.broadcast_to(own[:, start : start + 128], (128, 128)).T

    moved = moved_ref[pl.ds(pl.multiple_of(step * block, block), block), :]
    moved = jnp.concatenate([moved] * (vol_ref.shape[1] // 128), axis=1)
    near, far = pair(near0, near1), pair(far0, far1)
    value, _, bend = taylor(near + far)
    _, slope, _ = taylor(sign_ref[0] * (near - far))
    misfit_ref[...] = value + moved * (slope + 0.5 * moved * bend) - 2.0 * vol_ref[...]


def finish(where, sign, fields, streams, voxels, slabs):
    rows, columns = voxels.shape
    block = 128
    half = pl.BlockSpec((block, columns // 2), lambda i: (i, 0))
    full = pl.BlockSpec((block, columns), lambda i: (i, 0))
    return pl.pallas_call(
        functools.partial(final_kernel, slabs),
        grid=(rows // block,),
        in_specs=[SMEM, SMEM, pl.BlockSpec(fields.shape, lambda i: (0, 0)), half, half, half, half, full],
        out_specs=[pl.BlockSpec((1, rows), lambda i: (0, 0)), full],
        out_shape=[
            jax.ShapeDtypeStruct((1, rows), jnp.float32),
            jax.ShapeDtypeStruct((rows, columns), jnp.float32),
        ],
        scratch_shapes=[pltpu.VMEM((rows, 128), jnp.float32)],
        compiler_params=LIMIT,
        name="finish",
    )(where, sign, fields, *streams, voxels)


def swapped(block, axis):
    return lax.all_to_all(block, axis, split_axis=0, concat_axis=0, tiled=True)


def on_device(volume, velocity0, fetch_slab, fetch_row, modulus_class, modulus_table):
    voxels = volume[0]
    rows = voxels.shape[0]
    slabs = lax.axis_size("slab")
    scans = lax.axis_size("scan")
    capacity = max(2, 3 * rows // (2 * slabs))
    scan = lax.axis_index("scan")
    inner = (scan == 1) | (scan == 2)
    sign = jnp.where(scan % 2 == 0, 1.0, -1.0).astype(jnp.float32).reshape(1)

    names = fetch_slab[0, :, :, 0] * rows + fetch_row[0]
    partner = lax.ppermute(names[1], "scan", [(1, 0), (2, 1)]) + lax.ppermute(
        names[0], "scan", [(1, 2), (2, 3)]
    )
    own = jnp.where(scan % 2 == 0, names[0], names[1])
    tables, places = requests(jnp.stack([partner, own]), slabs, capacity)
    asked = swapped(tables.reshape(2, slabs, capacity).transpose(1, 0, 2), "slab")
    asked = asked.transpose(1, 0, 2).reshape(2, slabs * capacity)

    left, right = prefilter(voxels)
    near_left = lax.ppermute(left, "scan", [(1, 0), (2, 3)])
    near_right = lax.ppermute(right, "scan", [(1, 0), (2, 3), (0, 1), (3, 2)])

    def fetched(source, wanted, place):
        picked = jnp.take(source, wanted, axis=0).reshape(slabs, capacity, source.shape[1])
        arrived = swapped(picked, "slab").reshape(slabs * capacity, source.shape[1])
        return jnp.take(arrived, place, axis=0)

    first = fetched(left, asked[0], places[0])
    back_left = lax.ppermute(first, "scan", [(0, 1), (1, 2)])
    fore_left = lax.ppermute(first, "scan", [(2, 1), (3, 2)])
    second = fetched(
        jnp.where(inner, right, near_left),
        jnp.where(inner, asked[0], asked[1]),
        jnp.where(inner, places[0], places[1]),
    )
    far_right = lax.ppermute(second, "scan", [(1, 2), (2, 1)])
    third = fetched(near_right, asked[1], places[1])

    near_half = jnp.where(inner, jnp.where(scan == 1, back_left, fore_left), second)
    far_half = jnp.where(scan == 1, fore_left, back_left)
    streams = (near_half, third, far_half, far_right)

    classes = lax.broadcasted_iota(jnp.int32, (modulus_table.shape[0], 1), 0)
    weight = jnp.sum(jnp.where(modulus_class == classes, modulus_table[:, None], 0.0), axis=0)
    stiffness = jnp.sqrt(weight)

    sums = row_sums(sign, streams, voxels)
    payload = jnp.concatenate([sums, velocity0, stiffness[None]], axis=0).reshape(1, FIELDS * rows)
    everywhere = swapped(
        jnp.broadcast_to(payload, (scans * slabs, FIELDS * rows)), ("scan", "slab")
    )
    where = (scan * slabs + lax.axis_index("slab")).astype(jnp.int32).reshape(1)
    velocity, misfit = finish(where, sign, everywhere, streams, voxels, slabs)
    return velocity, misfit[None]


def solution(mesh):
    return jax.shard_map(
        on_device,
        mesh=mesh,
        in_specs=(
            P("scan", "slab", None),
            P("scan", "slab"),
            P("scan", None, "slab", None),
            P("scan", None, "slab"),
            P("scan", "slab"),
            P(),
        ),
        out_specs=(P("scan", "slab"), P("scan", "slab", None)),
        check_vma=False,
    )
```

```python
import functools
import math

import jax
import jax.numpy as jnp
from jax import lax
from jax.experimental import pallas as pl
from jax.experimental.pallas import tpu as pltpu
from jax.sharding import PartitionSpec as P

Y = 1024
BAND = 32
ITERS = 2
FIELDS = 8
HINT = 16
VMEM = pl.BlockSpec(memory_space=pltpu.VMEM)
SMEM = pl.BlockSpec(memory_space=pltpu.SMEM)
LIMIT = pltpu.CompilerParams(vmem_limit_bytes=16 * 1024 * 1024)


def cost(flops, values):
    return pl.CostEstimate(flops=flops, bytes_accessed=4 * values, transcendentals=0)


def store_filter(rim, high_ref, low_ref):
    shape = high_ref.shape
    distance = jnp.abs(lax.broadcasted_iota(jnp.int32, shape, 0) - rim - lax.broadcasted_iota(jnp.int32, shape, 1))
    parity = 1.0 - 2.0 * (distance % 2).astype(jnp.float32)
    size = jnp.exp(distance.astype(jnp.float32) * math.log(2.0 - math.sqrt(3.0)))
    exact = jnp.where(distance <= BAND, math.sqrt(3.0) * parity * size, 0.0)
    high = exact.astype(jnp.bfloat16)
    high_ref[...] = high
    low_ref[...] = (exact - high.astype(jnp.float32)).astype(jnp.bfloat16)


def prefilter_kernel(width, rim, vol_ref, early_ref, left_ref, right_ref, high_ref, low_ref):
    columns = vol_ref.shape[1]
    half = columns // 2

    @pl.when(pl.program_id(0) == 0)
    def _():
        store_filter(rim, high_ref, low_ref)

    voxels = vol_ref[...]
    high = voxels.astype(jnp.bfloat16)
    low = (voxels - high.astype(jnp.float32)).astype(jnp.bfloat16)
    for start in range(0, columns, width):
        first, last = max(0, start - rim), min(columns, start + width + rim)
        top = first - (start - rim)
        rows = slice(top, top + last - first)
        dot = functools.partial(jnp.dot, preferred_element_type=jnp.float32)
        out = dot(high[:, first:last], low_ref[rows, :]) + dot(low[:, first:last], high_ref[rows, :])
        out = out + dot(high[:, first:last], high_ref[rows, :])
        if start < half:
            left_ref[:, start : start + width] = out
        else:
            right_ref[:, start - half : start - half + width] = out


def prefilter(voxels, early):
    rows, columns = voxels.shape
    width, rim, block = 256, 128, 256
    halves = jax.ShapeDtypeStruct((rows, columns // 2), jnp.float32)
    matrix = pltpu.VMEM((width + 2 * rim, width), jnp.bfloat16)
    return pl.pallas_call(
        functools.partial(prefilter_kernel, width, rim),
        grid=(rows // block,),
        in_specs=[pl.BlockSpec((block, columns), lambda i: (i, 0)), pl.BlockSpec(memory_space=pl.ANY)],
        out_specs=[pl.BlockSpec((block, columns // 2), lambda i: (i, 0))] * 2,
        out_shape=[halves, halves],
        scratch_shapes=[matrix, matrix],
        cost_estimate=cost(3 * 2 * rows * columns * (width + 2 * rim), 2 * rows * columns),
        compiler_params=LIMIT,
        name="prefilter",
    )(voxels, early)


def column(line):
    parts = [
        jnp.broadcast_to(line[:, start : start + 128], (128, 128)).T for start in range(0, line.shape[1], 128)
    ]
    return parts[0] if len(parts) == 1 else jnp.concatenate(parts, axis=0)


def request_kernel(devices, capacity, direct, at_ref, inner_ref, side_ref, inward_ref, own_ref, table_ref, place_ref):
    rows = own_ref.shape[1]
    before = lax.broadcasted_iota(jnp.int32, (rows, rows), 0)
    after = lax.broadcasted_iota(jnp.int32, (rows, rows), 1)
    earlier = jnp.where(before < after, 1.0, 0.0).astype(jnp.bfloat16)
    peers = lax.broadcasted_iota(jnp.int32, (devices, rows), 0)
    core = at_ref[0] % 2
    slots = lax.broadcasted_iota(jnp.int32, (128, rows), 0)
    against = (((1,), (1,)), ((), ()))
    side = side_ref[...]
    for number, name in enumerate((side, jnp.where(inner_ref[0] != 0, inward_ref[...], side), own_ref[...])):
        peer = name // rows
        row = name - peer * rows
        if direct:
            peer = 2 * (peer // 2) + (peer + core) % 2
        hit = jnp.where(peers == peer, 1.0, 0.0)
        running = jnp.dot(hit.astype(jnp.bfloat16), earlier, preferred_element_type=jnp.float32)
        slot = jnp.sum(hit * running, axis=0, keepdims=True).astype(jnp.int32)
        if direct:
            peer = peer % 2 + 2 * ((at_ref[0] // 2 - peer // 2 + devices // 2) % (devices // 2))
        place_ref[number] = column(peer * capacity + slot)
        taken = jnp.where(slots == slot, 1.0, 0.0).astype(jnp.bfloat16)
        upper = (hit * (row // 16).astype(jnp.float32)).astype(jnp.bfloat16)
        lower = (hit * (row % 16).astype(jnp.float32)).astype(jnp.bfloat16)
        found = 16.0 * lax.dot_general(upper, taken, against, preferred_element_type=jnp.float32)
        found = found + lax.dot_general(lower, taken, against, preferred_element_type=jnp.float32)
        table_ref[:, 128 * number : 128 * number + 128] = found.astype(jnp.int32)


def requests(at, inner, partners, own, devices, capacity, direct):
    rows = own.shape[1]
    return pl.pallas_call(
        functools.partial(request_kernel, devices, capacity, direct),
        in_specs=[SMEM, SMEM, VMEM, VMEM, VMEM],
        out_specs=[VMEM, VMEM],
        out_shape=[
            jax.ShapeDtypeStruct((devices, 3 * 128), jnp.int32),
            jax.ShapeDtypeStruct((3, rows, 128), jnp.int32),
        ],
        compiler_params=LIMIT,
        name="requests",
    )(at, inner, *partners, own)


def terms(values):
    high = values.astype(jnp.bfloat16)
    rest = values - high.astype(jnp.float32)
    middle = rest.astype(jnp.bfloat16)
    low = (rest - middle.astype(jnp.float32)).astype(jnp.bfloat16)
    return high, middle, low


def picked(chosen, parts):
    dot = functools.partial(jnp.dot, preferred_element_type=jnp.float32)
    return (dot(chosen, parts[2]) + dot(chosen, parts[1])) + dot(chosen, parts[0])


def pick_kernel(chips, capacity, number, inner_ref, at_ref, asked_ref, *refs):
    sources, outs, chosen_ref = refs[: -1 - chips], refs[-1 - chips : -1], refs[-1]
    rows = sources[0].shape[0]
    row = lax.broadcasted_iota(jnp.int32, (128, rows), 1)
    for core in range(2):
        for turn in range(chips):
            line = asked_ref[pl.ds(2 * ((at_ref[0] // 2 + turn) % chips) + core, 1), :]
            line = line[:, 128 * number : 128 * number + 128]
            wanted = jnp.concatenate([column(line)] * (rows // 128), axis=1)
            hit = jnp.where(wanted == row, 1.0, 0.0)[:capacity]
            chosen_ref[turn * capacity : (turn + 1) * capacity, :] = hit.astype(jnp.bfloat16)
        source = sources[core][...]
        if len(sources) > 2:
            source = jnp.where(inner_ref[0] != 0, source, sources[2 + core][...])
        rows_out = picked(chosen_ref[...], terms(source))
        for turn in range(chips):
            outs[turn][core * capacity : (core + 1) * capacity, :] = rows_out[
                turn * capacity : (turn + 1) * capacity
            ]


def pick(inner, at, asked, number, sources, chips, capacity):
    rows, width = sources[0].shape
    block = jax.ShapeDtypeStruct((2 * capacity, width), jnp.float32)
    return pl.pallas_call(
        functools.partial(pick_kernel, chips, capacity, number),
        in_specs=[SMEM, SMEM] + [VMEM] * (1 + len(sources)),
        out_specs=[VMEM] * chips,
        out_shape=[block] * chips,
        scratch_shapes=[pltpu.VMEM((chips * capacity, rows), jnp.bfloat16)],
        cost_estimate=cost(HINT * 12 * chips * capacity * rows * width, 5 * rows * width),
        compiler_params=LIMIT,
        name="pick",
    )(inner, at, asked, *sources)


def store_terms(blocks, terms_ref):
    start = 0
    for block in blocks:
        for number, part in enumerate(terms(block[...])):
            terms_ref[number, start : start + block.shape[0], :] = part
        start += block.shape[0]


def placed(place, terms_ref):
    count = terms_ref.shape[1]
    lane = lax.broadcasted_iota(jnp.int32, place.shape, 1)
    chosen = [jnp.where(place - start == lane, 1.0, 0.0) for start in range(0, count, 128)]
    chosen = jnp.concatenate(chosen, axis=1).astype(jnp.bfloat16)
    return picked(chosen, [terms_ref[number] for number in range(3)])


def place_kernel(place_ref, *refs):
    blocks, out_ref, terms_ref = refs[:-2], refs[-2], refs[-1]

    @pl.when(pl.program_id(0) == 0)
    def _():
        store_terms(blocks, terms_ref)

    out_ref[...] = placed(place_ref[0], terms_ref)


def place(number, places, blocks):
    rows = places.shape[1]
    width = blocks[0].shape[1]
    total = sum(block.shape[0] for block in blocks)
    step = 256
    whole = [pl.BlockSpec(block.shape, lambda i: (0, 0)) for block in blocks]
    return pl.pallas_call(
        place_kernel,
        grid=(rows // step,),
        in_specs=[pl.BlockSpec((1, step, 128), lambda i: (number, i, 0))] + whole,
        out_specs=pl.BlockSpec((step, width), lambda i: (i, 0)),
        out_shape=jax.ShapeDtypeStruct((rows, width), jnp.float32),
        scratch_shapes=[pltpu.VMEM((3, total, width), jnp.bfloat16)],
        cost_estimate=cost(HINT * 3 * 2 * total * rows * width, 3 * rows * width),
        compiler_params=LIMIT,
        name="place",
    )(places, *blocks)


def taylor(coeffs):
    columns = coeffs.shape[1]
    lane = lax.broadcasted_iota(jnp.int32, coeffs.shape, 1)
    before = jnp.where(lane == 0, 0.0, pltpu.roll(coeffs, 1, 1))
    after = jnp.where(lane == columns - 1, 0.0, pltpu.roll(coeffs, columns - 1, 1))
    bend = after - 2.0 * coeffs + before
    return (before + 4.0 * coeffs + after) * (1.0 / 6.0), 0.5 * (after - before), bend


def lanes(values):
    rows, columns = values.shape
    total = values[:, 0:128]
    for start in range(128, columns, 128):
        total = total + values[:, start : start + 128]
    sums = [jnp.sum(total[start : start + 128].T, axis=0, keepdims=True) for start in range(0, rows, 128)]
    return jnp.concatenate(sums, axis=1)


def row_sums(sign, near, far, voxels, counted):
    kept = [jnp.where(counted, part, 0.0) for part in (*taylor(near), *taylor(far), voxels)]
    value, slope, bend, other_value, other_slope, other_bend, voxels = kept
    value = value - voxels
    other_value = other_value - voxels
    slope = sign * slope
    other_slope = -sign * other_slope
    c0 = slope * slope + other_slope * other_slope
    return (
        lanes(slope * value + other_slope * other_value),
        lanes(c0 + bend * value + other_bend * other_value),
        lanes(c0),
        lanes(2.0 * (slope * bend + other_slope * other_bend)),
        lanes(bend * bend + other_bend * other_bend),
    )


def left_sums_kernel(sign_ref, table_ref, near_ref, far_ref, vol_ref, start_ref, class_ref, out_ref):
    counted = lax.broadcasted_iota(jnp.int32, near_ref.shape, 1) < near_ref.shape[1] - 1
    lines = row_sums(sign_ref[0], near_ref[...], far_ref[...], vol_ref[...], counted)
    for number, line in enumerate(lines):
        out_ref[number : number + 1, :] = line
    weight = jnp.zeros(start_ref.shape, jnp.float32)
    for kind in range(table_ref.shape[0]):
        weight = jnp.where(class_ref[...] == kind, table_ref[kind], weight)
    out_ref[5:6, :] = start_ref[...]
    out_ref[6:7, :] = jnp.sqrt(weight)
    out_ref[7:8, :] = jnp.zeros(start_ref.shape, jnp.float32)


def left_sums(sign, table, near, far, voxels, start, classes):
    rows, half = near.shape
    step = 256
    block = pl.BlockSpec((step, half), lambda i: (i, 0))
    line = pl.BlockSpec((1, step), lambda i: (0, i))
    return pl.pallas_call(
        left_sums_kernel,
        grid=(rows // step,),
        in_specs=[SMEM, SMEM, block, block, block, line, line],
        out_specs=pl.BlockSpec((FIELDS, step), lambda i: (0, i)),
        out_shape=jax.ShapeDtypeStruct((FIELDS, rows), jnp.float32),
        cost_estimate=cost(60 * rows * half, 6 * rows * half),
        compiler_params=LIMIT,
        name="left_sums",
    )(sign, table, near, far, voxels, start, classes)


def right_sums_kernel(
    inner_ref, sign_ref, place_ref, near_rim, far_rim, vol_rim, hop_ref, vol_ref, so_far_ref, *refs
):
    blocks, fields_ref, third_ref, terms_ref = refs[:-3], refs[-3], refs[-2], refs[-1]

    @pl.when(pl.program_id(0) == 0)
    def _():
        store_terms(blocks, terms_ref)

    third = placed(place_ref[0], terms_ref)
    third_ref[...] = third
    inner = inner_ref[0] != 0
    near = jnp.concatenate([near_rim[...], jnp.where(inner, hop_ref[...], third)], axis=1)
    far = jnp.concatenate([far_rim[...], jnp.where(inner, third, 0.0)], axis=1)
    voxels = jnp.concatenate([vol_rim[...], vol_ref[...]], axis=1)
    counted = lax.broadcasted_iota(jnp.int32, far.shape, 1) >= 127
    for number, line in enumerate(row_sums(sign_ref[0], near, far, voxels, counted)):
        fields_ref[number : number + 1, :] = so_far_ref[number : number + 1, :] + line
    fields_ref[5:8, :] = so_far_ref[5:8, :]


def right_sums(inner, sign, places, near, far, voxels, hop, so_far, blocks):
    rows, half = near.shape
    step = 256
    total = sum(block.shape[0] for block in blocks)
    rim = pl.BlockSpec((step, 128), lambda i: (i, half // 128 - 1))
    block = pl.BlockSpec((step, half), lambda i: (i, 0))
    whole = [pl.BlockSpec(part.shape, lambda i: (0, 0)) for part in blocks]
    fields = pl.BlockSpec((FIELDS, step), lambda i: (0, i))
    return pl.pallas_call(
        right_sums_kernel,
        grid=(rows // step,),
        in_specs=[
            SMEM,
            SMEM,
            pl.BlockSpec((1, step, 128), lambda i: (2, i, 0)),
            rim,
            rim,
            rim,
            block,
            pl.BlockSpec((step, half), lambda i: (i, 1)),
            fields,
            *whole,
        ],
        out_specs=[fields, block],
        out_shape=[
            jax.ShapeDtypeStruct((FIELDS, rows), jnp.float32),
            jax.ShapeDtypeStruct((rows, half), jnp.float32),
        ],
        scratch_shapes=[pltpu.VMEM((3, total, half), jnp.bfloat16)],
        cost_estimate=cost(3 * 2 * total * rows * half, 5 * rows * half),
        compiler_params=LIMIT,
        name="right_sums",
    )(inner, sign, places, near, far, voxels, hop, voxels, so_far, *blocks)


def plane_stencil(field):
    slabs, rows = field.shape
    hops = Y // rows
    slab = lax.broadcasted_iota(jnp.int32, field.shape, 0)
    row = lax.broadcasted_iota(jnp.int32, field.shape, 1)

    def moved(cells, by):
        kept = slab >= by if by > 0 else slab < slabs + by
        return jnp.where(kept, pltpu.roll(cells, by % slabs, 0), 0.0)

    low = pltpu.roll(field, 1, 1)
    high = pltpu.roll(field, rows - 1, 1)
    low = jnp.where(row == 0, moved(low, 1), low)
    high = jnp.where(row == rows - 1, moved(high, -1), high)
    return 4.0 * field - low - high - moved(field, hops) - moved(field, -hops)


def total(parts):
    return jnp.sum(functools.reduce(jnp.add, parts), keepdims=True)


def iterate(groups):
    velocities = [group[5] for group in groups]
    for _ in range(ITERS):
        uppers, lowers, directions = [], [], []
        for (l0, l1, c0, c1, c2, _, stiffness, _), velocity in zip(groups, velocities):
            linear = l0 + velocity * (l1 + velocity * (0.75 * c1 + velocity * (0.5 * c2)))
            curvature = c0 + velocity * (c1 + velocity * c2)
            gradient = linear + stiffness * plane_stencil(stiffness * velocity)
            direction = gradient / (curvature + 4.0 * stiffness * stiffness)
            scaled = stiffness * direction
            uppers.append(direction * gradient)
            lowers.append(curvature * direction * direction + scaled * plane_stencil(scaled))
            directions.append(direction)
        alpha = total(uppers) / total(lowers)
        velocities = [velocity - alpha * direction for velocity, direction in zip(velocities, directions)]
    return velocities[0]


def final_kernel(scans, at_ref, inner_ref, sign_ref, *refs):
    fields_refs = refs[:scans]
    near0, far0, hop, third, vol_ref, velocity_ref, misfit_ref, moved_ref = refs[scans:]
    step = pl.program_id(0)
    rows = velocity_ref.shape[1]
    block = vol_ref.shape[0]

    @pl.when(step == 0)
    def _():
        groups = [[ref[:, i, :] for i in range(FIELDS)] for ref in fields_refs]
        velocity = iterate(groups)
        slab = lax.broadcasted_iota(jnp.int32, velocity.shape, 0)
        own = jnp.sum(jnp.where(slab == at_ref[0], velocity, 0.0), axis=0, keepdims=True)
        velocity_ref[...] = own
        moved_ref[...] = column(own)

    moved = moved_ref[pl.ds(pl.multiple_of(step * block, block), block), :]
    moved = jnp.concatenate([moved] * (vol_ref.shape[1] // 128), axis=1)
    inner = inner_ref[0] != 0
    near = jnp.concatenate([near0[...], jnp.where(inner, hop[...], third[...])], axis=1)
    far = jnp.concatenate([far0[...], jnp.where(inner, third[...], 0.0)], axis=1)
    value, _, bend = taylor(near + far)
    _, slope, _ = taylor(sign_ref[0] * (near - far))
    misfit_ref[...] = value + moved * (slope + 0.5 * moved * bend) - 2.0 * vol_ref[...]


def finish(at, inner, sign, groups, streams, voxels):
    rows, columns = voxels.shape
    step = 256
    half = pl.BlockSpec((step, columns // 2), lambda i: (i, 0))
    full = pl.BlockSpec((step, columns), lambda i: (i, 0))
    whole = [pl.BlockSpec(group.shape, lambda i: (0, 0, 0)) for group in groups]
    return pl.pallas_call(
        functools.partial(final_kernel, len(groups)),
        grid=(rows // step,),
        in_specs=[SMEM, SMEM, SMEM, *whole, half, half, half, half, full],
        out_specs=[pl.BlockSpec((1, rows), lambda i: (0, 0)), full],
        out_shape=[
            jax.ShapeDtypeStruct((1, rows), jnp.float32),
            jax.ShapeDtypeStruct((rows, columns), jnp.float32),
        ],
        scratch_shapes=[pltpu.VMEM((rows, 128), jnp.float32)],
        compiler_params=LIMIT,
        name="finish",
    )(at, inner, sign, *groups, *streams, voxels)


def swapped(block, axis):
    return lax.all_to_all(block, axis, split_axis=0, concat_axis=0, tiled=True)


def after(block, *earlier):
    return lax.optimization_barrier((block, *earlier))[0]


ORDER = (2, 1, 3)


def on_device(volume, velocity0, fetch_slab, fetch_row, modulus_class, modulus_table):
    voxels = volume[0]
    rows = voxels.shape[0]
    slabs = lax.axis_size("slab")
    scans = lax.axis_size("scan")
    capacity = max(2, 3 * rows // (2 * slabs))
    direct = slabs == 8
    scan = lax.axis_index("scan")
    slab = lax.axis_index("slab")
    at = slab.astype(jnp.int32).reshape(1)
    inner = ((scan == 1) | (scan == 2)).astype(jnp.int32).reshape(1)
    sign = jnp.where(scan % 2 == 0, 1.0, -1.0).astype(jnp.float32).reshape(1)
    sides = [(0, 1), (1, 0), (2, 3), (3, 2)]
    middle = [(1, 2), (2, 1)]

    names = fetch_slab[0, :, :, 0] * rows + fetch_row[0]
    lent = jnp.where(scan % 2 == 0, names[0:1], names[1:2])
    own = jnp.where(scan < 2, names[0:1], names[1:2])
    partners = [lax.ppermute(lent, "scan", sides), lax.ppermute(own, "scan", middle)]
    table, places = requests(at, inner, partners, own, slabs, capacity, direct)
    chips = slabs // 2
    if direct:
        same_core = [list(range(core, slabs, 2)) for core in range(2)]
        asked = lax.all_to_all(table, "slab", 0, 0, axis_index_groups=same_core, tiled=True)
    else:
        asked = swapped(table, "slab")

    def other_core(block):
        return lax.ppermute(block, "slab", [(p, p ^ 1) for p in range(slabs)]) if direct else block

    left, right = prefilter(voxels, names)
    left, right, _ = lax.optimization_barrier((left, right, table))
    left_other, right_other = other_core(left), other_core(right)
    from_inner = lax.ppermute(right, "scan", [(1, 0), (2, 3)])
    from_middle = lax.ppermute(right, "scan", middle)

    def picks(number, sources):
        if direct:
            return pick(inner, at, asked, number, sources, chips, capacity)
        source = sources[0] if len(sources) == 2 else jnp.where(inner[0] != 0, sources[0], sources[2])
        wanted = asked[:, 128 * number : 128 * number + capacity]
        return [jnp.take(source, wanted.reshape(-1), axis=0)]

    sent = []

    def fetched(blocks):
        if not direct:
            arrived = swapped(blocks[0].reshape(slabs, capacity, -1), "slab")
            return [arrived.reshape(slabs * capacity, -1)]
        arrived = [blocks[0]] + [None] * (chips - 1)
        for turn in ORDER:
            held = sent[-3:-2]
            block = after(blocks[turn], *held) if held else blocks[turn]
            route = [(p, (p + 2 * turn) % slabs) for p in range(slabs)]
            arrived[turn] = lax.ppermute(block, "slab", route)
            sent.append(arrived[turn])
        return arrived

    arrived = fetched(picks(0, [left, left_other]))
    first = place(0, places, arrived)
    lender = jnp.where(inner == 1, after(from_middle, *arrived), from_inner)
    near = lax.ppermute(first, "scan", sides)
    arrived = fetched(picks(1, [left, left_other, right, right_other]))
    blocks = picks(2, [lender, other_core(lender)])
    second = place(1, places, [after(arrived[0], blocks[0]), *arrived[1:]])
    hop = lax.ppermute(second, "scan", [(0, 1), (3, 2)])
    far = lax.ppermute(second, "scan", middle)
    arrived = fetched(blocks)
    so_far = left_sums(sign, modulus_table, near, far, voxels, velocity0, modulus_class)
    sums, third = right_sums(inner, sign, places, near, far, voxels, hop, so_far, arrived)

    column_sums = swapped(jnp.broadcast_to(sums[None], (slabs, FIELDS, rows)), "slab")
    groups = [column_sums]
    for turn in range(1, scans):
        groups.append(lax.ppermute(column_sums, "scan", [(p, (p + turn) % scans) for p in range(scans)]))
    velocity, misfit = finish(
        at, inner, sign, groups, (near, far, hop, third), after(voxels, sums)
    )
    return velocity, misfit[None]


def solution(mesh):
    return jax.shard_map(
        on_device,
        mesh=mesh,
        in_specs=(
            P("scan", "slab", None),
            P("scan", "slab"),
            P("scan", None, "slab", None),
            P("scan", None, "slab"),
            P("scan", "slab"),
            P(),
        ),
        out_specs=(P("scan", "slab"), P("scan", "slab", None)),
        check_vma=False,
    )
```

```python
import functools
import math

import jax
import jax.numpy as jnp
from jax import lax
from jax.experimental import pallas as pl
from jax.experimental.pallas import tpu as pltpu
from jax.sharding import PartitionSpec as P

Y = 1024
BAND = 32
ITERS = 2
FIELDS = 8
HINT = 16
VMEM = pl.BlockSpec(memory_space=pltpu.VMEM)
SMEM = pl.BlockSpec(memory_space=pltpu.SMEM)
LIMIT = pltpu.CompilerParams(vmem_limit_bytes=20 * 1024 * 1024)


def cost(flops, values):
    return pl.CostEstimate(flops=flops, bytes_accessed=4 * values, transcendentals=0)


def store_filter(rim, high_ref, low_ref):
    shape = high_ref.shape
    distance = jnp.abs(lax.broadcasted_iota(jnp.int32, shape, 0) - rim - lax.broadcasted_iota(jnp.int32, shape, 1))
    parity = 1.0 - 2.0 * (distance % 2).astype(jnp.float32)
    size = jnp.exp(distance.astype(jnp.float32) * math.log(2.0 - math.sqrt(3.0)))
    exact = jnp.where(distance <= BAND, math.sqrt(3.0) * parity * size, 0.0)
    high = exact.astype(jnp.bfloat16)
    high_ref[...] = high
    low_ref[...] = (exact - high.astype(jnp.float32)).astype(jnp.bfloat16)


def prefilter_kernel(width, rim, vol_ref, early_ref, left_ref, right_ref, high_ref, low_ref, held_ref, sent):
    rows, columns = vol_ref.shape
    half = columns // 2
    steps = held_ref.shape[0]
    block = rows // steps
    copies = [
        pltpu.make_async_copy(vol_ref.at[pl.ds(number * block, block)], held_ref.at[number], sent.at[number])
        for number in range(steps)
    ]
    for copy in copies:
        copy.start()
    store_filter(rim, high_ref, low_ref)
    for number, copy in enumerate(copies):
        copy.wait()
        at = slice(number * block, (number + 1) * block)
        voxels = held_ref[number]
        high = voxels.astype(jnp.bfloat16)
        low = (voxels - high.astype(jnp.float32)).astype(jnp.bfloat16)
        for start in range(0, columns, width):
            first, last = max(0, start - rim), min(columns, start + width + rim)
            top = first - (start - rim)
            band = slice(top, top + last - first)
            dot = functools.partial(jnp.dot, preferred_element_type=jnp.float32)
            out = dot(high[:, first:last], low_ref[band, :]) + dot(low[:, first:last], high_ref[band, :])
            out = out + dot(high[:, first:last], high_ref[band, :])
            if start < half:
                left_ref[at, start : start + width] = out
            else:
                right_ref[at, start - half : start - half + width] = out


def prefilter(voxels, early):
    rows, columns = voxels.shape
    width, rim, steps = 256, 128, 2
    halves = jax.ShapeDtypeStruct((rows, columns // 2), jnp.float32)
    matrix = pltpu.VMEM((width + 2 * rim, width), jnp.bfloat16)
    anywhere = pl.BlockSpec(memory_space=pl.ANY)
    return pl.pallas_call(
        functools.partial(prefilter_kernel, width, rim),
        in_specs=[pl.BlockSpec(memory_space=pltpu.HBM), anywhere],
        out_specs=[VMEM, VMEM],
        out_shape=[halves, halves],
        scratch_shapes=[
            matrix,
            matrix,
            pltpu.VMEM((steps, rows // steps, columns), jnp.float32),
            pltpu.SemaphoreType.DMA((steps,)),
        ],
        cost_estimate=cost(3 * 2 * rows * columns * (width + 2 * rim), 2 * rows * columns),
        compiler_params=LIMIT,
        name="prefilter",
    )(voxels, early)


def column(line):
    parts = [
        jnp.broadcast_to(line[:, start : start + 128], (128, 128)).T for start in range(0, line.shape[1], 128)
    ]
    return parts[0] if len(parts) == 1 else jnp.concatenate(parts, axis=0)


def request_kernel(devices, capacity, direct, inner_ref, at_ref, side_ref, inward_ref, own_ref, place_ref, *table_refs):
    rows = own_ref.shape[1]
    before = lax.broadcasted_iota(jnp.int32, (rows, rows), 0)
    after = lax.broadcasted_iota(jnp.int32, (rows, rows), 1)
    earlier = jnp.where(before < after, 1.0, 0.0).astype(jnp.bfloat16)
    peers = lax.broadcasted_iota(jnp.int32, (devices, rows), 0)
    chip, core, chips = at_ref[0] // 2, at_ref[0] % 2, devices // 2
    slots = lax.broadcasted_iota(jnp.int32, (128, rows), 0)
    against = (((1,), (1,)), ((), ()))
    side = side_ref[...]
    for number, name in enumerate((side, jnp.where(inner_ref[0] != 0, inward_ref[...], side), own_ref[...])):
        peer = name // rows
        row = name - peer * rows
        turn = peer
        if direct:
            other = (peer + core) % 2
            turn = 2 * ((chip - peer // 2 + chips) % chips) + other
            peer = 2 * ((peer // 2 - chip + chips) % chips) + other
        hit = jnp.where(peers == peer, 1.0, 0.0)
        running = jnp.dot(hit.astype(jnp.bfloat16), earlier, preferred_element_type=jnp.float32)
        slot = jnp.sum(hit * running, axis=0, keepdims=True).astype(jnp.int32)
        place_ref[number] = column(turn * capacity + slot)
        taken = jnp.where(slots == slot, 1.0, 0.0).astype(jnp.bfloat16)
        upper = (hit * (row // 16).astype(jnp.float32)).astype(jnp.bfloat16)
        lower = (hit * (row % 16).astype(jnp.float32)).astype(jnp.bfloat16)
        found = 16.0 * lax.dot_general(upper, taken, against, preferred_element_type=jnp.float32)
        found = found + lax.dot_general(lower, taken, against, preferred_element_type=jnp.float32)
        share = devices // len(table_refs)
        for turn, table_ref in enumerate(table_refs):
            lines = found[turn * share : (turn + 1) * share].astype(jnp.int32)
            table_ref[:, 128 * number : 128 * number + 128] = lines


def requests(inner, at, side, inward, own, devices, capacity, direct):
    rows = own.shape[1]
    parts = devices // 2 if direct else 1
    places, *tables = pl.pallas_call(
        functools.partial(request_kernel, devices, capacity, direct),
        in_specs=[SMEM, SMEM, VMEM, VMEM, VMEM],
        out_specs=[VMEM] * (1 + parts),
        out_shape=[jax.ShapeDtypeStruct((3, rows, 128), jnp.int32)]
        + [jax.ShapeDtypeStruct((devices // parts, 3 * 128), jnp.int32)] * parts,
        compiler_params=LIMIT,
        name="requests",
    )(inner, at, side, inward, own)
    return places, tables


def terms(values):
    high = values.astype(jnp.bfloat16)
    rest = values - high.astype(jnp.float32)
    middle = rest.astype(jnp.bfloat16)
    low = (rest - middle.astype(jnp.float32)).astype(jnp.bfloat16)
    return high, middle, low


def picked(chosen, parts):
    dot = functools.partial(jnp.dot, preferred_element_type=jnp.float32)
    return (dot(chosen, parts[2]) + dot(chosen, parts[1])) + dot(chosen, parts[0])


def pick_kernel(chips, capacity, number, inner_ref, *refs):
    asked_refs, refs = refs[:chips], refs[chips:]
    sources, outs, chosen_ref = refs[: -1 - chips], refs[-1 - chips : -1], refs[-1]
    rows = sources[0].shape[0]
    row = lax.broadcasted_iota(jnp.int32, (128, rows), 1)
    for core in range(2):
        for turn in range(chips):
            back = (chips - turn) % chips
            line = asked_refs[back][core : core + 1, 128 * number : 128 * number + 128]
            wanted = jnp.concatenate([column(line)] * (rows // 128), axis=1)
            hit = jnp.where(wanted == row, 1.0, 0.0)[:capacity]
            chosen_ref[turn * capacity : (turn + 1) * capacity, :] = hit.astype(jnp.bfloat16)
        source = sources[core][...]
        if len(sources) > 2:
            source = jnp.where(inner_ref[0] != 0, source, sources[2 + core][...])
        rows_out = picked(chosen_ref[...], terms(source))
        for turn in range(chips):
            outs[turn][core * capacity : (core + 1) * capacity, :] = rows_out[
                turn * capacity : (turn + 1) * capacity
            ]


def pick(inner, asked, number, sources, chips, capacity):
    rows, width = sources[0].shape
    block = jax.ShapeDtypeStruct((2 * capacity, width), jnp.float32)
    return pl.pallas_call(
        functools.partial(pick_kernel, chips, capacity, number),
        in_specs=[SMEM] + [VMEM] * (len(asked) + len(sources)),
        out_specs=[VMEM] * chips,
        out_shape=[block] * chips,
        scratch_shapes=[pltpu.VMEM((chips * capacity, rows), jnp.bfloat16)],
        cost_estimate=cost(HINT * 12 * chips * capacity * rows * width, 5 * rows * width),
        compiler_params=LIMIT,
        name="pick",
    )(inner, *asked, *sources)


def store_terms(blocks, terms_ref):
    start = 0
    for block in blocks:
        for number, part in enumerate(terms(block[...])):
            terms_ref[number, start : start + block.shape[0], :] = part
        start += block.shape[0]


def placed(place, terms_ref):
    count = terms_ref.shape[1]
    lane = lax.broadcasted_iota(jnp.int32, place.shape, 1)
    chosen = [jnp.where(place - start == lane, 1.0, 0.0) for start in range(0, count, 128)]
    chosen = jnp.concatenate(chosen, axis=1).astype(jnp.bfloat16)
    return picked(chosen, [terms_ref[number] for number in range(3)])


def place_kernel(number, place_ref, *refs):
    blocks, out_ref, terms_ref = refs[:-2], refs[-2], refs[-1]
    store_terms(blocks, terms_ref)
    out_ref[...] = placed(place_ref[number], terms_ref)


def place(number, places, blocks):
    rows = places.shape[1]
    width = blocks[0].shape[1]
    total = sum(block.shape[0] for block in blocks)
    return pl.pallas_call(
        functools.partial(place_kernel, number),
        in_specs=[VMEM] * (1 + len(blocks)),
        out_specs=VMEM,
        out_shape=jax.ShapeDtypeStruct((rows, width), jnp.float32),
        scratch_shapes=[pltpu.VMEM((3, total, width), jnp.bfloat16)],
        cost_estimate=cost(HINT * 3 * 2 * total * rows * width, 3 * rows * width),
        compiler_params=LIMIT,
        name="place",
    )(places, *blocks)


def on_tile(values, at, change):
    parts = [values[:, :at], change(values[:, at : at + 128]), values[:, at + 128 :]]
    return jnp.concatenate([part for part in parts if part.shape[1]], axis=1)


def cleared(lane):
    return lambda tile: jnp.where(lax.broadcasted_iota(jnp.int32, tile.shape, 1) == lane, 0.0, tile)


def before_of(values):
    return on_tile(pltpu.roll(values, 1, 1), 0, cleared(0))


def after_of(values):
    columns = values.shape[1]
    return on_tile(pltpu.roll(values, columns - 1, 1), columns - 128, cleared(127))


def taylor(coeffs, counted):
    before, after = before_of(coeffs), after_of(coeffs)
    bend = after - 2.0 * coeffs + before
    return counted(coeffs + bend * (1.0 / 6.0)), counted(0.5 * (after - before)), counted(bend)


def lanes(values):
    rows, columns = values.shape
    total = values[:, 0:128]
    for start in range(128, columns, 128):
        total = total + values[:, start : start + 128]
    sums = [jnp.sum(total[start : start + 128].T, axis=0, keepdims=True) for start in range(0, rows, 128)]
    return jnp.concatenate(sums, axis=1)


def row_sums(sign, near, far, voxels, counted):
    voxels = counted(voxels)
    value, slope, bend = taylor(near, counted)
    other_value, other_slope, other_bend = taylor(far, counted)
    value = value - voxels
    other_value = other_value - voxels
    slope = sign * slope
    other_slope = -sign * other_slope
    c0 = slope * slope + other_slope * other_slope
    return (
        lanes(slope * value + other_slope * other_value),
        lanes(c0 + bend * value + other_bend * other_value),
        lanes(c0),
        lanes(2.0 * (slope * bend + other_slope * other_bend)),
        lanes(bend * bend + other_bend * other_bend),
    )


STEP = 128


def left_sums_kernel(sign_ref, table_ref, near_ref, far_ref, vol_ref, start_ref, class_ref, out_ref):
    rows, half = near_ref.shape

    def counted(values):
        return on_tile(values, half - 128, cleared(127))

    for start in range(0, rows, STEP):
        at = slice(start, start + STEP)
        lines = row_sums(sign_ref[0], near_ref[at], far_ref[at], vol_ref[at, :half], counted)
        for number, line in enumerate(lines):
            out_ref[number : number + 1, at] = line
    weight = jnp.zeros(start_ref.shape, jnp.float32)
    for kind in range(table_ref.shape[0]):
        weight = jnp.where(class_ref[...] == kind, table_ref[kind], weight)
    out_ref[5:6, :] = start_ref[...]
    out_ref[6:7, :] = jnp.sqrt(weight)
    out_ref[7:8, :] = jnp.zeros(start_ref.shape, jnp.float32)


def left_sums(sign, table, near, far, voxels, start, classes):
    rows, half = near.shape
    return pl.pallas_call(
        left_sums_kernel,
        in_specs=[SMEM, SMEM] + [VMEM] * 5,
        out_specs=VMEM,
        out_shape=jax.ShapeDtypeStruct((FIELDS, rows), jnp.float32),
        cost_estimate=cost(60 * rows * half, 6 * rows * half),
        compiler_params=LIMIT,
        name="left_sums",
    )(sign, table, near, far, voxels, start, classes)


def right_sums_kernel(inner_ref, sign_ref, place_ref, near_ref, far_ref, hop_ref, vol_ref, so_far_ref, *refs):
    blocks, fields_ref, third_ref, terms_ref = refs[:-3], refs[-3], refs[-2], refs[-1]
    rows, half = near_ref.shape
    inner = inner_ref[0] != 0
    store_terms(blocks, terms_ref)
    third_ref[...] = placed(place_ref[2], terms_ref)

    def counted(values):
        lane = lax.broadcasted_iota(jnp.int32, (STEP, 128), 1)
        return on_tile(values, 0, lambda tile: jnp.where(lane == 127, tile, 0.0))

    for start in range(0, rows, STEP):
        at = slice(start, start + STEP)
        third = third_ref[at]
        near = jnp.concatenate([near_ref[at, half - 128 :], jnp.where(inner, hop_ref[at], third)], axis=1)
        far = jnp.concatenate([far_ref[at, half - 128 :], jnp.where(inner, third, 0.0)], axis=1)
        lines = row_sums(sign_ref[0], near, far, vol_ref[at, half - 128 :], counted)
        for number, line in enumerate(lines):
            fields_ref[number : number + 1, at] = so_far_ref[number : number + 1, at] + line
    fields_ref[5:8, :] = so_far_ref[5:8, :]


def right_sums(inner, sign, places, near, far, hop, voxels, so_far, blocks):
    rows, half = near.shape
    total = sum(block.shape[0] for block in blocks)
    return pl.pallas_call(
        right_sums_kernel,
        in_specs=[SMEM, SMEM] + [VMEM] * (6 + len(blocks)),
        out_specs=[VMEM, VMEM],
        out_shape=[
            jax.ShapeDtypeStruct((FIELDS, rows), jnp.float32),
            jax.ShapeDtypeStruct((rows, half), jnp.float32),
        ],
        scratch_shapes=[pltpu.VMEM((3, total, half), jnp.bfloat16)],
        cost_estimate=cost(3 * 2 * total * rows * half, 5 * rows * half),
        compiler_params=LIMIT,
        name="right_sums",
    )(inner, sign, places, near, far, hop, voxels, so_far, *blocks)


def plane_stencil(field):
    slabs, rows = field.shape
    hops = Y // rows
    slab = lax.broadcasted_iota(jnp.int32, field.shape, 0)
    row = lax.broadcasted_iota(jnp.int32, field.shape, 1)

    def moved(cells, by):
        kept = slab >= by if by > 0 else slab < slabs + by
        return jnp.where(kept, pltpu.roll(cells, by % slabs, 0), 0.0)

    low = pltpu.roll(field, 1, 1)
    high = pltpu.roll(field, rows - 1, 1)
    low = jnp.where(row == 0, moved(low, 1), low)
    high = jnp.where(row == rows - 1, moved(high, -1), high)
    return 4.0 * field - low - high - moved(field, hops) - moved(field, -hops)


def total(parts):
    return jnp.sum(functools.reduce(jnp.add, parts), keepdims=True)


def iterate(groups):
    velocities = [group[5] for group in groups]
    for _ in range(ITERS):
        uppers, lowers, directions = [], [], []
        for (l0, l1, c0, c1, c2, _, stiffness, _), velocity in zip(groups, velocities):
            linear = l0 + velocity * (l1 + velocity * (0.75 * c1 + velocity * (0.5 * c2)))
            curvature = c0 + velocity * (c1 + velocity * c2)
            gradient = linear + stiffness * plane_stencil(stiffness * velocity)
            direction = gradient / (curvature + 4.0 * stiffness * stiffness)
            scaled = stiffness * direction
            uppers.append(direction * gradient)
            lowers.append(curvature * direction * direction + scaled * plane_stencil(scaled))
            directions.append(direction)
        alpha = total(uppers) / total(lowers)
        velocities = [velocity - alpha * direction for velocity, direction in zip(velocities, directions)]
    return velocities[0]


def final_kernel(chips, at_ref, inner_ref, sign_ref, *refs):
    fields_refs = refs[:-10]
    near_ref, far_ref, hop_ref, third_ref, vol_ref, velocity_ref, misfit_ref = refs[-10:-3]
    fields_ref, tile_ref, sent = refs[-3:]
    rows, half = near_ref.shape
    if chips:
        scans = len(fields_refs) // 2
        for number, ref in enumerate(fields_refs):
            core = (at_ref[0] + number // scans) % 2
            for turn in range(chips):
                slab = 2 * ((at_ref[0] // 2 - turn + chips) % chips) + core
                fields_ref[number % scans, slab] = ref[FIELDS * turn : FIELDS * turn + FIELDS, :]
        groups = [[fields_ref[scan, :, i, :] for i in range(FIELDS)] for scan in range(scans)]
    else:
        groups = [[ref[:, i, :] for i in range(FIELDS)] for ref in fields_refs]
    velocity = iterate(groups)
    slab = lax.broadcasted_iota(jnp.int32, velocity.shape, 0)
    own = jnp.sum(jnp.where(slab == at_ref[0], velocity, 0.0), axis=0, keepdims=True)
    velocity_ref[...] = own

    inner = inner_ref[0] != 0
    copies = []
    for number, start in enumerate(range(0, rows, STEP)):
        at = slice(start, start + STEP)
        moved = column(own[:, at])
        weight = 1.0 / 6.0 + 0.5 * moved * moved
        drift = (0.5 * sign_ref[0]) * moved
        wide = lambda tile: jnp.concatenate([tile] * (2 * half // 128), axis=1)
        up, down, middle = wide(weight + drift), wide(weight - drift), wide(1.0 - 2.0 * weight)
        third = third_ref[at]
        near = jnp.concatenate([near_ref[at], jnp.where(inner, hop_ref[at], third)], axis=1)
        far = jnp.concatenate([far_ref[at], jnp.where(inner, third, 0.0)], axis=1)
        after = after_of(up * near + down * far)
        before = before_of(down * near + up * far)
        tile_ref[number] = middle * (near + far) + after + before - 2.0 * vol_ref[at]
        copies.append(pltpu.make_async_copy(tile_ref.at[number], misfit_ref.at[pl.ds(start, STEP)], sent.at[number]))
        copies[-1].start()
    for copy in copies:
        copy.wait()


def finish(at, inner, sign, groups, streams, voxels, chips):
    rows, columns = voxels.shape
    steps = rows // STEP
    shape = (len(groups) // 2, 2 * chips, FIELDS, rows) if chips else (1, 1, 8, 128)
    return pl.pallas_call(
        functools.partial(final_kernel, chips),
        in_specs=[SMEM, SMEM, SMEM] + [VMEM] * (len(groups) + 5),
        out_specs=[VMEM, pl.BlockSpec(memory_space=pl.ANY)],
        out_shape=[
            jax.ShapeDtypeStruct((1, rows), jnp.float32),
            jax.ShapeDtypeStruct((rows, columns), jnp.float32),
        ],
        scratch_shapes=[
            pltpu.VMEM(shape, jnp.float32),
            pltpu.VMEM((steps, STEP, columns), jnp.float32),
            pltpu.SemaphoreType.DMA((steps,)),
        ],
        compiler_params=LIMIT,
        name="finish",
    )(at, inner, sign, *groups, *streams, voxels)


def swapped(block, axis):
    return lax.all_to_all(block, axis, split_axis=0, concat_axis=0, tiled=True)


def after(block, *earlier):
    return lax.optimization_barrier((block, *earlier))[0]


ORDER = (2, 1, 3)


def on_device(volume, velocity0, fetch_slab, fetch_row, modulus_class, modulus_table):
    voxels = volume[0]
    rows = voxels.shape[0]
    slabs = lax.axis_size("slab")
    scans = lax.axis_size("scan")
    capacity = max(2, 3 * rows // (2 * slabs))
    direct = slabs == 8
    scan = lax.axis_index("scan")
    slab = lax.axis_index("slab")
    at = slab.astype(jnp.int32).reshape(1)
    inner = ((scan == 1) | (scan == 2)).astype(jnp.int32).reshape(1)
    sign = jnp.where(scan % 2 == 0, 1.0, -1.0).astype(jnp.float32).reshape(1)
    sides = [(0, 1), (1, 0), (2, 3), (3, 2)]
    middle = [(1, 2), (2, 1)]

    names = fetch_slab[0, :, :, 0] * rows + fetch_row[0]
    lent = jnp.where(scan % 2 == 0, names[0:1], names[1:2])
    own = jnp.where(scan < 2, names[0:1], names[1:2])
    side, inward = lax.ppermute(lent, "scan", sides), lax.ppermute(own, "scan", middle)
    places, tables = requests(inner, at, side, inward, own, slabs, capacity, direct)
    chips = slabs // 2
    turns = [[(p, (p + 2 * turn) % slabs) for p in range(slabs)] for turn in range(chips)]
    if direct:
        asked = tables[:1] + [lax.ppermute(tables[turn], "slab", turns[turn]) for turn in range(1, chips)]
    else:
        asked = [swapped(tables[0], "slab")]

    def other_core(block):
        return lax.ppermute(block, "slab", [(p, p ^ 1) for p in range(slabs)]) if direct else block

    left, right = prefilter(voxels, names)
    left, right, _ = lax.optimization_barrier((left, right, tables[0]))
    left_other, right_other = other_core(left), other_core(right)
    from_inner = lax.ppermute(right, "scan", [(1, 0), (2, 3)])
    from_middle = lax.ppermute(right, "scan", middle)

    def picks(number, sources):
        if direct:
            return pick(inner, asked, number, sources, chips, capacity)
        source = sources[0] if len(sources) == 2 else jnp.where(inner[0] != 0, sources[0], sources[2])
        wanted = asked[0][:, 128 * number : 128 * number + capacity]
        return [jnp.take(source, wanted.reshape(-1), axis=0)]

    sent = []

    def fetched(blocks):
        if not direct:
            arrived = swapped(blocks[0].reshape(slabs, capacity, -1), "slab")
            return [arrived.reshape(slabs * capacity, -1)]
        arrived = [blocks[0]] + [None] * (chips - 1)
        for turn in ORDER:
            held = sent[-3:-2]
            block = after(blocks[turn], *held) if held else blocks[turn]
            arrived[turn] = lax.ppermute(block, "slab", turns[turn])
            sent.append(arrived[turn])
        return arrived

    blocks = picks(0, [left, left_other])
    arrived = fetched(blocks)
    first = place(0, places, arrived)
    lender = jnp.where(inner == 1, after(from_middle, *arrived), from_inner)
    near = lax.ppermute(first, "scan", sides)
    arrived = fetched(picks(1, [left, left_other, right, right_other]))
    blocks = picks(2, [lender, other_core(lender)])
    second = place(1, places, [after(arrived[0], blocks[0]), *arrived[1:]])
    hop = lax.ppermute(second, "scan", [(0, 1), (3, 2)])
    far = lax.ppermute(second, "scan", middle)
    arrived = fetched(blocks)
    so_far = left_sums(sign, modulus_table, near, far, voxels, velocity0, modulus_class)
    sums, third = right_sums(inner, sign, places, near, far, hop, voxels, so_far, arrived)

    def scans_of(block):
        routes = [[(p, (p + turn) % scans) for p in range(scans)] for turn in range(1, scans)]
        return [block] + [lax.ppermute(block, "scan", route) for route in routes]

    if direct:
        line = jnp.concatenate([sums] + [lax.ppermute(sums, "slab", route) for route in turns[1:]], axis=0)
        groups = scans_of(line)
        groups += [other_core(group) for group in groups]
    else:
        groups = scans_of(swapped(jnp.broadcast_to(sums[None], (slabs, FIELDS, rows)), "slab"))
    velocity, misfit = finish(
        at, inner, sign, groups, (near, far, hop, third), after(voxels, sums), chips if direct else 0
    )
    return velocity, misfit[None]


def solution(mesh):
    return jax.shard_map(
        on_device,
        mesh=mesh,
        in_specs=(
            P("scan", "slab", None),
            P("scan", "slab"),
            P("scan", None, "slab", None),
            P("scan", None, "slab"),
            P("scan", "slab"),
            P(),
        ),
        out_specs=(P("scan", "slab"), P("scan", "slab", None)),
        check_vma=False,
    )
```

```python
import functools
import math

import jax
import jax.numpy as jnp
from jax import lax
from jax.experimental import pallas as pl
from jax.experimental.pallas import tpu as pltpu
from jax.sharding import PartitionSpec as P

Y = 1024
BAND = 32
ITERS = 2
FIELDS = 8
HINT = 16
VMEM = pl.BlockSpec(memory_space=pltpu.VMEM)
SMEM = pl.BlockSpec(memory_space=pltpu.SMEM)
LIMIT = pltpu.CompilerParams(vmem_limit_bytes=20 * 1024 * 1024)


def cost(flops, values):
    return pl.CostEstimate(flops=flops, bytes_accessed=4 * values, transcendentals=0)


def store_filter(rim, high_ref, low_ref):
    shape = high_ref.shape
    distance = jnp.abs(lax.broadcasted_iota(jnp.int32, shape, 0) - rim - lax.broadcasted_iota(jnp.int32, shape, 1))
    parity = 1.0 - 2.0 * (distance % 2).astype(jnp.float32)
    size = jnp.exp(distance.astype(jnp.float32) * math.log(2.0 - math.sqrt(3.0)))
    exact = jnp.where(distance <= BAND, math.sqrt(3.0) * parity * size, 0.0)
    high = exact.astype(jnp.bfloat16)
    high_ref[...] = high
    low_ref[...] = (exact - high.astype(jnp.float32)).astype(jnp.bfloat16)


def prefilter_kernel(width, rim, vol_ref, early_ref, left_ref, right_ref, high_ref, low_ref, held_ref, sent):
    rows, columns = vol_ref.shape
    half = columns // 2
    steps = held_ref.shape[0]
    block = rows // steps
    copies = [
        pltpu.make_async_copy(vol_ref.at[pl.ds(number * block, block)], held_ref.at[number], sent.at[number])
        for number in range(steps)
    ]
    for copy in copies:
        copy.start()
    store_filter(rim, high_ref, low_ref)
    for number, copy in enumerate(copies):
        copy.wait()
        at = slice(number * block, (number + 1) * block)
        voxels = held_ref[number]
        high = voxels.astype(jnp.bfloat16)
        low = (voxels - high.astype(jnp.float32)).astype(jnp.bfloat16)
        for start in range(0, columns, width):
            first, last = max(0, start - rim), min(columns, start + width + rim)
            top = first - (start - rim)
            band = slice(top, top + last - first)
            dot = functools.partial(jnp.dot, preferred_element_type=jnp.float32)
            out = dot(high[:, first:last], low_ref[band, :]) + dot(low[:, first:last], high_ref[band, :])
            out = out + dot(high[:, first:last], high_ref[band, :])
            if start < half:
                left_ref[at, start : start + width] = out
            else:
                right_ref[at, start - half : start - half + width] = out


def prefilter(voxels, early):
    rows, columns = voxels.shape
    width, rim, steps = 256, 128, 2
    halves = jax.ShapeDtypeStruct((rows, columns // 2), jnp.float32)
    matrix = pltpu.VMEM((width + 2 * rim, width), jnp.bfloat16)
    anywhere = pl.BlockSpec(memory_space=pl.ANY)
    return pl.pallas_call(
        functools.partial(prefilter_kernel, width, rim),
        in_specs=[pl.BlockSpec(memory_space=pltpu.HBM), anywhere],
        out_specs=[VMEM, VMEM],
        out_shape=[halves, halves],
        scratch_shapes=[
            matrix,
            matrix,
            pltpu.VMEM((steps, rows // steps, columns), jnp.float32),
            pltpu.SemaphoreType.DMA((steps,)),
        ],
        cost_estimate=cost(3 * 2 * rows * columns * (width + 2 * rim), 2 * rows * columns),
        compiler_params=LIMIT,
        name="prefilter",
    )(voxels, early)


def column(line):
    parts = [
        jnp.broadcast_to(line[:, start : start + 128], (128, 128)).T for start in range(0, line.shape[1], 128)
    ]
    return parts[0] if len(parts) == 1 else jnp.concatenate(parts, axis=0)


def request_kernel(devices, capacity, direct, inner_ref, at_ref, side_ref, inward_ref, own_ref, place_ref, *table_refs):
    rows = own_ref.shape[1]
    before = lax.broadcasted_iota(jnp.int32, (rows, rows), 0)
    after = lax.broadcasted_iota(jnp.int32, (rows, rows), 1)
    earlier = jnp.where(before < after, 1.0, 0.0).astype(jnp.bfloat16)
    peers = lax.broadcasted_iota(jnp.int32, (devices, rows), 0)
    chip, core, chips = at_ref[0] // 2, at_ref[0] % 2, devices // 2
    slots = lax.broadcasted_iota(jnp.int32, (128, rows), 0)
    against = (((1,), (1,)), ((), ()))
    side = side_ref[...]
    for number, name in enumerate((side, jnp.where(inner_ref[0] != 0, inward_ref[...], side), own_ref[...])):
        peer = name // rows
        row = name - peer * rows
        turn = peer
        if direct:
            other = (peer + core) % 2
            turn = 2 * ((chip - peer // 2 + chips) % chips) + other
            peer = 2 * ((peer // 2 - chip + chips) % chips) + other
        hit = jnp.where(peers == peer, 1.0, 0.0)
        running = jnp.dot(hit.astype(jnp.bfloat16), earlier, preferred_element_type=jnp.float32)
        slot = jnp.sum(hit * running, axis=0, keepdims=True).astype(jnp.int32)
        place_ref[number] = column(turn * capacity + slot)
        taken = jnp.where(slots == slot, 1.0, 0.0).astype(jnp.bfloat16)
        upper = (hit * (row // 16).astype(jnp.float32)).astype(jnp.bfloat16)
        lower = (hit * (row % 16).astype(jnp.float32)).astype(jnp.bfloat16)
        found = 16.0 * lax.dot_general(upper, taken, against, preferred_element_type=jnp.float32)
        found = found + lax.dot_general(lower, taken, against, preferred_element_type=jnp.float32)
        share = devices // len(table_refs)
        for turn, table_ref in enumerate(table_refs):
            lines = found[turn * share : (turn + 1) * share].astype(jnp.int32)
            table_ref[:, 128 * number : 128 * number + 128] = lines


def requests(inner, at, side, inward, own, devices, capacity, direct):
    rows = own.shape[1]
    parts = devices // 2 if direct else 1
    places, *tables = pl.pallas_call(
        functools.partial(request_kernel, devices, capacity, direct),
        in_specs=[SMEM, SMEM, VMEM, VMEM, VMEM],
        out_specs=[VMEM] * (1 + parts),
        out_shape=[jax.ShapeDtypeStruct((3, rows, 128), jnp.int32)]
        + [jax.ShapeDtypeStruct((devices // parts, 3 * 128), jnp.int32)] * parts,
        compiler_params=LIMIT,
        name="requests",
    )(inner, at, side, inward, own)
    return places, tables


def terms(values):
    high = values.astype(jnp.bfloat16)
    rest = values - high.astype(jnp.float32)
    middle = rest.astype(jnp.bfloat16)
    low = (rest - middle.astype(jnp.float32)).astype(jnp.bfloat16)
    return high, middle, low


def picked(chosen, parts):
    dot = functools.partial(jnp.dot, preferred_element_type=jnp.float32)
    return (dot(chosen, parts[2]) + dot(chosen, parts[1])) + dot(chosen, parts[0])


def pick_kernel(chips, capacity, number, inner_ref, *refs):
    asked_refs, refs = refs[:chips], refs[chips:]
    sources, outs, chosen_ref = refs[: -1 - chips], refs[-1 - chips : -1], refs[-1]
    rows = sources[0].shape[0]
    row = lax.broadcasted_iota(jnp.int32, (128, rows), 1)
    for core in range(2):
        for turn in range(chips):
            back = (chips - turn) % chips
            line = asked_refs[back][core : core + 1, 128 * number : 128 * number + 128]
            wanted = jnp.concatenate([column(line)] * (rows // 128), axis=1)
            hit = jnp.where(wanted == row, 1.0, 0.0)[:capacity]
            chosen_ref[turn * capacity : (turn + 1) * capacity, :] = hit.astype(jnp.bfloat16)
        source = sources[core][...]
        if len(sources) > 2:
            source = jnp.where(inner_ref[0] != 0, source, sources[2 + core][...])
        rows_out = picked(chosen_ref[...], terms(source))
        for turn in range(chips):
            outs[turn][core * capacity : (core + 1) * capacity, :] = rows_out[
                turn * capacity : (turn + 1) * capacity
            ]


def pick(inner, asked, number, sources, chips, capacity):
    rows, width = sources[0].shape
    block = jax.ShapeDtypeStruct((2 * capacity, width), jnp.float32)
    return pl.pallas_call(
        functools.partial(pick_kernel, chips, capacity, number),
        in_specs=[SMEM] + [VMEM] * (len(asked) + len(sources)),
        out_specs=[VMEM] * chips,
        out_shape=[block] * chips,
        scratch_shapes=[pltpu.VMEM((chips * capacity, rows), jnp.bfloat16)],
        cost_estimate=cost(HINT * 12 * chips * capacity * rows * width, 5 * rows * width),
        compiler_params=LIMIT,
        name="pick",
    )(inner, *asked, *sources)


def store_terms(blocks, terms_ref):
    start = 0
    for block in blocks:
        for number, part in enumerate(terms(block[...])):
            terms_ref[number, start : start + block.shape[0], :] = part
        start += block.shape[0]


def placed(place, terms_ref):
    count = terms_ref.shape[1]
    lane = lax.broadcasted_iota(jnp.int32, place.shape, 1)
    chosen = [jnp.where(place - start == lane, 1.0, 0.0) for start in range(0, count, 128)]
    chosen = jnp.concatenate(chosen, axis=1).astype(jnp.bfloat16)
    return picked(chosen, [terms_ref[number] for number in range(3)])


def place_kernel(number, place_ref, *refs):
    blocks, out_ref, terms_ref = refs[:-2], refs[-2], refs[-1]
    store_terms(blocks, terms_ref)
    out_ref[...] = placed(place_ref[number], terms_ref)


def place(number, places, blocks):
    rows = places.shape[1]
    width = blocks[0].shape[1]
    total = sum(block.shape[0] for block in blocks)
    return pl.pallas_call(
        functools.partial(place_kernel, number),
        in_specs=[VMEM] * (1 + len(blocks)),
        out_specs=VMEM,
        out_shape=jax.ShapeDtypeStruct((rows, width), jnp.float32),
        scratch_shapes=[pltpu.VMEM((3, total, width), jnp.bfloat16)],
        cost_estimate=cost(HINT * 3 * 2 * total * rows * width, 3 * rows * width),
        compiler_params=LIMIT,
        name="place",
    )(places, *blocks)


def on_tile(values, at, change):
    parts = [values[:, :at], change(values[:, at : at + 128]), values[:, at + 128 :]]
    return jnp.concatenate([part for part in parts if part.shape[1]], axis=1)


def cleared(lane):
    return lambda tile: jnp.where(lax.broadcasted_iota(jnp.int32, tile.shape, 1) == lane, 0.0, tile)


def before_of(values):
    return on_tile(pltpu.roll(values, 1, 1), 0, cleared(0))


def after_of(values):
    columns = values.shape[1]
    return on_tile(pltpu.roll(values, columns - 1, 1), columns - 128, cleared(127))


def taylor(coeffs, counted):
    before, after = before_of(coeffs), after_of(coeffs)
    bend = after - 2.0 * coeffs + before
    return counted(coeffs + bend * (1.0 / 6.0)), counted(0.5 * (after - before)), counted(bend)


def lanes(values):
    rows, columns = values.shape
    total = values[:, 0:128]
    for start in range(128, columns, 128):
        total = total + values[:, start : start + 128]
    sums = [jnp.sum(total[start : start + 128].T, axis=0, keepdims=True) for start in range(0, rows, 128)]
    return jnp.concatenate(sums, axis=1)


def row_sums(sign, stream, voxels, counted):
    value, slope, bend = taylor(stream, counted)
    value = value - counted(voxels)
    slope = sign * slope
    c0 = slope * slope
    return (
        lanes(slope * value),
        lanes(c0 + bend * value),
        lanes(c0),
        lanes(2.0 * (slope * bend)),
        lanes(bend * bend),
    )


STEP = 128


def all_but_last(values):
    return on_tile(values, values.shape[1] - 128, cleared(127))


def near_sums_kernel(sign_ref, table_ref, near_ref, vol_ref, start_ref, class_ref, out_ref):
    rows, half = near_ref.shape
    for start in range(0, rows, STEP):
        at = slice(start, start + STEP)
        lines = row_sums(sign_ref[0], near_ref[at], vol_ref[at, :half], all_but_last)
        for number, line in enumerate(lines):
            out_ref[number : number + 1, at] = line
    weight = jnp.zeros(start_ref.shape, jnp.float32)
    for kind in range(table_ref.shape[0]):
        weight = jnp.where(class_ref[...] == kind, table_ref[kind], weight)
    out_ref[5:6, :] = start_ref[...]
    out_ref[6:7, :] = jnp.sqrt(weight)
    out_ref[7:8, :] = jnp.zeros(start_ref.shape, jnp.float32)


def near_sums(sign, table, near, voxels, start, classes):
    rows, half = near.shape
    return pl.pallas_call(
        near_sums_kernel,
        in_specs=[SMEM, SMEM] + [VMEM] * 4,
        out_specs=VMEM,
        out_shape=jax.ShapeDtypeStruct((FIELDS, rows), jnp.float32),
        cost_estimate=cost(HINT * 5000 * rows * half, 5 * rows * half),
        compiler_params=LIMIT,
        name="near_sums",
    )(sign, table, near, voxels, start, classes)


def far_sums_kernel(sign_ref, far_ref, vol_ref, so_far_ref, out_ref):
    rows, half = far_ref.shape
    for start in range(0, rows, STEP):
        at = slice(start, start + STEP)
        lines = row_sums(-sign_ref[0], far_ref[at], vol_ref[at, :half], all_but_last)
        for number, line in enumerate(lines):
            out_ref[number : number + 1, at] = so_far_ref[number : number + 1, at] + line
    out_ref[5:8, :] = so_far_ref[5:8, :]


def far_sums(sign, far, voxels, so_far):
    rows, half = far.shape
    return pl.pallas_call(
        far_sums_kernel,
        in_specs=[SMEM] + [VMEM] * 3,
        out_specs=VMEM,
        out_shape=jax.ShapeDtypeStruct((FIELDS, rows), jnp.float32),
        cost_estimate=cost(60 * rows * half, 5 * rows * half),
        compiler_params=LIMIT,
        name="far_sums",
    )(sign, far, voxels, so_far)


def right_sums_kernel(inner_ref, sign_ref, place_ref, near_ref, far_ref, hop_ref, vol_ref, so_far_ref, *refs):
    blocks, fields_ref, third_ref, terms_ref = refs[:-3], refs[-3], refs[-2], refs[-1]
    rows, half = near_ref.shape
    inner = inner_ref[0] != 0
    store_terms(blocks, terms_ref)
    third_ref[...] = placed(place_ref[2], terms_ref)

    def counted(values):
        lane = lax.broadcasted_iota(jnp.int32, (STEP, 128), 1)
        return on_tile(values, 0, lambda tile: jnp.where(lane == 127, tile, 0.0))

    for start in range(0, rows, STEP):
        at = slice(start, start + STEP)
        third = third_ref[at]
        near = jnp.concatenate([near_ref[at, half - 128 :], jnp.where(inner, hop_ref[at], third)], axis=1)
        far = jnp.concatenate([far_ref[at, half - 128 :], jnp.where(inner, third, 0.0)], axis=1)
        voxels = vol_ref[at, half - 128 :]
        lines = zip(row_sums(sign_ref[0], near, voxels, counted), row_sums(-sign_ref[0], far, voxels, counted))
        for number, (line, other) in enumerate(lines):
            fields_ref[number : number + 1, at] = so_far_ref[number : number + 1, at] + line + other
    fields_ref[5:8, :] = so_far_ref[5:8, :]


def right_sums(inner, sign, places, near, far, hop, voxels, so_far, blocks):
    rows, half = near.shape
    total = sum(block.shape[0] for block in blocks)
    return pl.pallas_call(
        right_sums_kernel,
        in_specs=[SMEM, SMEM] + [VMEM] * (6 + len(blocks)),
        out_specs=[VMEM, VMEM],
        out_shape=[
            jax.ShapeDtypeStruct((FIELDS, rows), jnp.float32),
            jax.ShapeDtypeStruct((rows, half), jnp.float32),
        ],
        scratch_shapes=[pltpu.VMEM((3, total, half), jnp.bfloat16)],
        cost_estimate=cost(3 * 2 * total * rows * half, 5 * rows * half),
        compiler_params=LIMIT,
        name="right_sums",
    )(inner, sign, places, near, far, hop, voxels, so_far, *blocks)


def plane_stencil(field):
    slabs, rows = field.shape
    hops = Y // rows
    slab = lax.broadcasted_iota(jnp.int32, field.shape, 0)
    row = lax.broadcasted_iota(jnp.int32, field.shape, 1)

    def moved(cells, by):
        kept = slab >= by if by > 0 else slab < slabs + by
        return jnp.where(kept, pltpu.roll(cells, by % slabs, 0), 0.0)

    low = pltpu.roll(field, 1, 1)
    high = pltpu.roll(field, rows - 1, 1)
    low = jnp.where(row == 0, moved(low, 1), low)
    high = jnp.where(row == rows - 1, moved(high, -1), high)
    return 4.0 * field - low - high - moved(field, hops) - moved(field, -hops)


def total(parts):
    return jnp.sum(functools.reduce(jnp.add, parts), keepdims=True)


def iterate(groups):
    velocities = [group[5] for group in groups]
    for _ in range(ITERS):
        uppers, lowers, directions = [], [], []
        for (l0, l1, c0, c1, c2, _, stiffness, _), velocity in zip(groups, velocities):
            linear = l0 + velocity * (l1 + velocity * (0.75 * c1 + velocity * (0.5 * c2)))
            curvature = c0 + velocity * (c1 + velocity * c2)
            gradient = linear + stiffness * plane_stencil(stiffness * velocity)
            direction = gradient / (curvature + 4.0 * stiffness * stiffness)
            scaled = stiffness * direction
            uppers.append(direction * gradient)
            lowers.append(curvature * direction * direction + scaled * plane_stencil(scaled))
            directions.append(direction)
        alpha = total(uppers) / total(lowers)
        velocities = [velocity - alpha * direction for velocity, direction in zip(velocities, directions)]
    return velocities[0]


def shape_kernel(inner_ref, sign_ref, near_ref, far_ref, hop_ref, third_ref, vol_ref, flat_ref, tilt_ref, curl_ref):
    inner = inner_ref[0] != 0
    for start in range(0, near_ref.shape[0], STEP):
        at = slice(start, start + STEP)
        third = third_ref[at]
        near = jnp.concatenate([near_ref[at], jnp.where(inner, hop_ref[at], third)], axis=1)
        far = jnp.concatenate([far_ref[at], jnp.where(inner, third, 0.0)], axis=1)
        both, drift = near + far, (0.5 * sign_ref[0]) * (near - far)
        bend = after_of(both) - 2.0 * both + before_of(both)
        flat_ref[at] = both + bend * (1.0 / 6.0) - 2.0 * vol_ref[at]
        tilt_ref[at] = after_of(drift) - before_of(drift)
        curl_ref[at] = 0.5 * bend


def shapes(inner, sign, streams, voxels):
    rows, columns = voxels.shape
    return pl.pallas_call(
        shape_kernel,
        in_specs=[SMEM, SMEM] + [VMEM] * 5,
        out_specs=[VMEM] * 3,
        out_shape=[jax.ShapeDtypeStruct((rows, columns), jnp.float32)] * 3,
        cost_estimate=cost(30 * rows * columns, 7 * rows * columns),
        compiler_params=LIMIT,
        name="shapes",
    )(inner, sign, *streams, voxels)


def final_kernel(chips, at_ref, *refs):
    fields_refs = refs[:-8]
    flat_ref, tilt_ref, curl_ref, velocity_ref, misfit_ref, fields_ref, tile_ref, sent = refs[-8:]
    rows, columns = flat_ref.shape
    if chips:
        scans = len(fields_refs) // 2
        for number, ref in enumerate(fields_refs):
            core = (at_ref[0] + number // scans) % 2
            for turn in range(chips):
                slab = 2 * ((at_ref[0] // 2 - turn + chips) % chips) + core
                fields_ref[number % scans, slab] = ref[FIELDS * turn : FIELDS * turn + FIELDS, :]
        groups = [[fields_ref[scan, :, i, :] for i in range(FIELDS)] for scan in range(scans)]
    else:
        groups = [[ref[:, i, :] for i in range(FIELDS)] for ref in fields_refs]
    velocity = iterate(groups)
    slab = lax.broadcasted_iota(jnp.int32, velocity.shape, 0)
    own = jnp.sum(jnp.where(slab == at_ref[0], velocity, 0.0), axis=0, keepdims=True)
    velocity_ref[...] = own

    copies = []
    for number, start in enumerate(range(0, rows, STEP)):
        at = slice(start, start + STEP)
        moved = jnp.concatenate([column(own[:, at])] * (columns // 128), axis=1)
        tile_ref[number] = flat_ref[at] + moved * (tilt_ref[at] + moved * curl_ref[at])
        copies.append(pltpu.make_async_copy(tile_ref.at[number], misfit_ref.at[pl.ds(start, STEP)], sent.at[number]))
        copies[-1].start()
    for copy in copies:
        copy.wait()


def finish(at, groups, parts, chips):
    rows, columns = parts[0].shape
    steps = rows // STEP
    shape = (len(groups) // 2, 2 * chips, FIELDS, rows) if chips else (1, 1, 8, 128)
    return pl.pallas_call(
        functools.partial(final_kernel, chips),
        in_specs=[SMEM] + [VMEM] * (len(groups) + 3),
        out_specs=[VMEM, pl.BlockSpec(memory_space=pl.ANY)],
        out_shape=[
            jax.ShapeDtypeStruct((1, rows), jnp.float32),
            jax.ShapeDtypeStruct((rows, columns), jnp.float32),
        ],
        scratch_shapes=[
            pltpu.VMEM(shape, jnp.float32),
            pltpu.VMEM((steps, STEP, columns), jnp.float32),
            pltpu.SemaphoreType.DMA((steps,)),
        ],
        compiler_params=LIMIT,
        name="finish",
    )(at, *groups, *parts)


def swapped(block, axis):
    return lax.all_to_all(block, axis, split_axis=0, concat_axis=0, tiled=True)


def after(block, *earlier):
    return lax.optimization_barrier((block, *earlier))[0]


def on_device(volume, velocity0, fetch_slab, fetch_row, modulus_class, modulus_table):
    voxels = volume[0]
    rows = voxels.shape[0]
    slabs = lax.axis_size("slab")
    scans = lax.axis_size("scan")
    capacity = max(2, 3 * rows // (2 * slabs))
    direct = slabs == 8
    scan = lax.axis_index("scan")
    slab = lax.axis_index("slab")
    at = slab.astype(jnp.int32).reshape(1)
    inner = ((scan == 1) | (scan == 2)).astype(jnp.int32).reshape(1)
    sign = jnp.where(scan % 2 == 0, 1.0, -1.0).astype(jnp.float32).reshape(1)
    sides = [(0, 1), (1, 0), (2, 3), (3, 2)]
    middle = [(1, 2), (2, 1)]

    names = fetch_slab[0, :, :, 0] * rows + fetch_row[0]
    lent = jnp.where(scan % 2 == 0, names[0:1], names[1:2])
    own = jnp.where(scan < 2, names[0:1], names[1:2])
    side, inward = lax.ppermute(lent, "scan", sides), lax.ppermute(own, "scan", middle)
    places, tables = requests(inner, at, side, inward, own, slabs, capacity, direct)
    chips = slabs // 2
    turns = [[(p, (p + 2 * turn) % slabs) for p in range(slabs)] for turn in range(chips)]
    if direct:
        asked = tables[:1] + [lax.ppermute(tables[turn], "slab", turns[turn]) for turn in range(1, chips)]
    else:
        asked = [swapped(tables[0], "slab")]

    def other_core(block):
        return lax.ppermute(block, "slab", [(p, p ^ 1) for p in range(slabs)]) if direct else block

    left, right = prefilter(voxels, names)
    left, right, _ = lax.optimization_barrier((left, right, tables[0]))
    left_other, right_other = other_core(left), other_core(right)
    from_inner = lax.ppermute(right, "scan", [(1, 0), (2, 3)])
    from_middle = lax.ppermute(right, "scan", middle)

    def picks(number, sources):
        if direct:
            return pick(inner, asked, number, sources, chips, capacity)
        source = sources[0] if len(sources) == 2 else jnp.where(inner[0] != 0, sources[0], sources[2])
        wanted = asked[0][:, 128 * number : 128 * number + capacity]
        return [jnp.take(source, wanted.reshape(-1), axis=0)]

    sent = []

    def fetched(blocks, order, before_last=()):
        if not direct:
            arrived = swapped(blocks[0].reshape(slabs, capacity, -1), "slab")
            return [arrived.reshape(slabs * capacity, -1)]
        arrived = [blocks[0]] + [None] * (chips - 1)
        for turn in order:
            held = sent[-3:-2] + (list(before_last) if turn == order[-1] else [])
            block = after(blocks[turn], *held) if held else blocks[turn]
            arrived[turn] = lax.ppermute(block, "slab", turns[turn])
            sent.append(arrived[turn])
        return arrived

    order = (2, 1, 3)
    arrived = fetched(picks(0, [left, left_other]), order)
    first = place(0, places, arrived)
    lender = jnp.where(inner == 1, after(from_middle, *arrived), from_inner)
    near = lax.ppermute(first, "scan", sides)
    arrived2 = fetched(picks(1, [left, left_other, right, right_other]), order)
    blocks = picks(2, [lender, other_core(lender)])
    second = place(1, places, [after(arrived2[0], blocks[0]), *arrived2[1:]])
    order = (1, 2, 3)
    arrived = fetched(blocks, order)
    hop = lax.ppermute(second, "scan", [(0, 1), (3, 2)])
    far = lax.ppermute(second, "scan", middle)
    begun = arrived[1:2] if direct else arrived
    so_far = near_sums(sign, modulus_table, after(near, *begun), voxels, velocity0, modulus_class)
    so_far = far_sums(sign, far, voxels, so_far)
    sums, third = right_sums(inner, sign, places, near, far, hop, voxels, so_far, arrived)

    def scans_of(block):
        routes = [[(p, (p + turn) % scans) for p in range(scans)] for turn in range(1, scans)]
        return [block] + [lax.ppermute(block, "scan", route) for route in routes]

    parts = shapes(inner, sign, (near, far, hop, third), voxels)
    if direct:
        line = jnp.concatenate([sums] + [lax.ppermute(sums, "slab", route) for route in turns[1:]], axis=0)
        line = after(line, parts[0])
        groups = scans_of(line)
        groups += [other_core(group) for group in groups]
    else:
        groups = scans_of(swapped(jnp.broadcast_to(sums[None], (slabs, FIELDS, rows)), "slab"))
    velocity, misfit = finish(at, groups, parts, chips if direct else 0)
    return velocity, misfit[None]


def solution(mesh):
    return jax.shard_map(
        on_device,
        mesh=mesh,
        in_specs=(
            P("scan", "slab", None),
            P("scan", "slab"),
            P("scan", None, "slab", None),
            P("scan", None, "slab"),
            P("scan", "slab"),
            P(),
        ),
        out_specs=(P("scan", "slab"), P("scan", "slab", None)),
        check_vma=False,
    )
```

```python
import functools
import math

import jax
import jax.numpy as jnp
from jax import lax
from jax.experimental import pallas as pl
from jax.experimental.pallas import tpu as pltpu
from jax.sharding import PartitionSpec as P

Y = 1024
BAND = 32
ITERS = 2
FIELDS = 8
HINT = 16
VMEM = pl.BlockSpec(memory_space=pltpu.VMEM)
SMEM = pl.BlockSpec(memory_space=pltpu.SMEM)
LIMIT = pltpu.CompilerParams(vmem_limit_bytes=20 * 1024 * 1024)


def cost(flops, values):
    return pl.CostEstimate(flops=flops, bytes_accessed=4 * values, transcendentals=0)


def store_filter(rim, high_ref, low_ref):
    shape = high_ref.shape
    distance = jnp.abs(lax.broadcasted_iota(jnp.int32, shape, 0) - rim - lax.broadcasted_iota(jnp.int32, shape, 1))
    parity = 1.0 - 2.0 * (distance % 2).astype(jnp.float32)
    size = jnp.exp(distance.astype(jnp.float32) * math.log(2.0 - math.sqrt(3.0)))
    exact = jnp.where(distance <= BAND, math.sqrt(3.0) * parity * size, 0.0)
    high = exact.astype(jnp.bfloat16)
    high_ref[...] = high
    low_ref[...] = (exact - high.astype(jnp.float32)).astype(jnp.bfloat16)


def prefilter_kernel(width, rim, vol_ref, early_ref, left_ref, right_ref, high_ref, low_ref, held_ref, sent):
    rows, columns = vol_ref.shape
    half = columns // 2
    steps = held_ref.shape[0]
    block = rows // steps
    copies = [
        pltpu.make_async_copy(vol_ref.at[pl.ds(number * block, block)], held_ref.at[number], sent.at[number])
        for number in range(steps)
    ]
    for copy in copies:
        copy.start()
    store_filter(rim, high_ref, low_ref)
    for number, copy in enumerate(copies):
        copy.wait()
        at = slice(number * block, (number + 1) * block)
        voxels = held_ref[number]
        high = voxels.astype(jnp.bfloat16)
        low = (voxels - high.astype(jnp.float32)).astype(jnp.bfloat16)
        for start in range(0, columns, width):
            first, last = max(0, start - rim), min(columns, start + width + rim)
            top = first - (start - rim)
            band = slice(top, top + last - first)
            dot = functools.partial(jnp.dot, preferred_element_type=jnp.float32)
            out = dot(high[:, first:last], low_ref[band, :]) + dot(low[:, first:last], high_ref[band, :])
            out = out + dot(high[:, first:last], high_ref[band, :])
            if start < half:
                left_ref[at, start : start + width] = out
            else:
                right_ref[at, start - half : start - half + width] = out


def prefilter(voxels, early):
    rows, columns = voxels.shape
    width, rim, steps = 256, 128, 2
    halves = jax.ShapeDtypeStruct((rows, columns // 2), jnp.float32)
    matrix = pltpu.VMEM((width + 2 * rim, width), jnp.bfloat16)
    anywhere = pl.BlockSpec(memory_space=pl.ANY)
    return pl.pallas_call(
        functools.partial(prefilter_kernel, width, rim),
        in_specs=[pl.BlockSpec(memory_space=pltpu.HBM), anywhere],
        out_specs=[VMEM, VMEM],
        out_shape=[halves, halves],
        scratch_shapes=[
            matrix,
            matrix,
            pltpu.VMEM((steps, rows // steps, columns), jnp.float32),
            pltpu.SemaphoreType.DMA((steps,)),
        ],
        cost_estimate=cost(3 * 2 * rows * columns * (width + 2 * rim), 2 * rows * columns),
        compiler_params=LIMIT,
        name="prefilter",
    )(voxels, early)


def column(line):
    parts = [
        jnp.broadcast_to(line[:, start : start + 128], (128, 128)).T for start in range(0, line.shape[1], 128)
    ]
    return parts[0] if len(parts) == 1 else jnp.concatenate(parts, axis=0)


def request_kernel(devices, capacity, direct, inner_ref, at_ref, side_ref, inward_ref, own_ref, place_ref, *table_refs):
    rows = own_ref.shape[1]
    before = lax.broadcasted_iota(jnp.int32, (rows, rows), 0)
    after = lax.broadcasted_iota(jnp.int32, (rows, rows), 1)
    earlier = jnp.where(before < after, 1.0, 0.0).astype(jnp.bfloat16)
    peers = lax.broadcasted_iota(jnp.int32, (devices, rows), 0)
    chip, core, chips = at_ref[0] // 2, at_ref[0] % 2, devices // 2
    slots = lax.broadcasted_iota(jnp.int32, (128, rows), 0)
    against = (((1,), (1,)), ((), ()))
    side = side_ref[...]
    for number, name in enumerate((side, jnp.where(inner_ref[0] != 0, inward_ref[...], side), own_ref[...])):
        peer = name // rows
        row = name - peer * rows
        turn = peer
        if direct:
            other = (peer + core) % 2
            turn = 2 * ((chip - peer // 2 + chips) % chips) + other
            peer = 2 * ((peer // 2 - chip + chips) % chips) + other
        hit = jnp.where(peers == peer, 1.0, 0.0)
        running = jnp.dot(hit.astype(jnp.bfloat16), earlier, preferred_element_type=jnp.float32)
        slot = jnp.sum(hit * running, axis=0, keepdims=True).astype(jnp.int32)
        place_ref[number] = column(turn * capacity + slot)
        taken = jnp.where(slots == slot, 1.0, 0.0).astype(jnp.bfloat16)
        upper = (hit * (row // 16).astype(jnp.float32)).astype(jnp.bfloat16)
        lower = (hit * (row % 16).astype(jnp.float32)).astype(jnp.bfloat16)
        found = 16.0 * lax.dot_general(upper, taken, against, preferred_element_type=jnp.float32)
        found = found + lax.dot_general(lower, taken, against, preferred_element_type=jnp.float32)
        share = devices // len(table_refs)
        for turn, table_ref in enumerate(table_refs):
            lines = found[turn * share : (turn + 1) * share].astype(jnp.int32)
            table_ref[:, 128 * number : 128 * number + 128] = lines


def requests(inner, at, side, inward, own, devices, capacity, direct):
    rows = own.shape[1]
    parts = devices // 2 if direct else 1
    places, *tables = pl.pallas_call(
        functools.partial(request_kernel, devices, capacity, direct),
        in_specs=[SMEM, SMEM, VMEM, VMEM, VMEM],
        out_specs=[VMEM] * (1 + parts),
        out_shape=[jax.ShapeDtypeStruct((3, rows, 128), jnp.int32)]
        + [jax.ShapeDtypeStruct((devices // parts, 3 * 128), jnp.int32)] * parts,
        compiler_params=LIMIT,
        name="requests",
    )(inner, at, side, inward, own)
    return places, tables


def terms(values):
    high = values.astype(jnp.bfloat16)
    rest = values - high.astype(jnp.float32)
    middle = rest.astype(jnp.bfloat16)
    low = (rest - middle.astype(jnp.float32)).astype(jnp.bfloat16)
    return high, middle, low


def picked(chosen, parts):
    dot = functools.partial(jnp.dot, preferred_element_type=jnp.float32)
    return (dot(chosen, parts[2]) + dot(chosen, parts[1])) + dot(chosen, parts[0])


def pick_kernel(chips, capacity, number, inner_ref, *refs):
    asked_refs, refs = refs[:chips], refs[chips:]
    sources, outs, chosen_ref = refs[: -1 - chips], refs[-1 - chips : -1], refs[-1]
    rows = sources[0].shape[0]
    row = lax.broadcasted_iota(jnp.int32, (128, rows), 1)
    for core in range(2):
        for turn in range(chips):
            back = (chips - turn) % chips
            line = asked_refs[back][core : core + 1, 128 * number : 128 * number + 128]
            wanted = jnp.concatenate([column(line)] * (rows // 128), axis=1)
            hit = jnp.where(wanted == row, 1.0, 0.0)[:capacity]
            chosen_ref[turn * capacity : (turn + 1) * capacity, :] = hit.astype(jnp.bfloat16)
        source = sources[core][...]
        if len(sources) > 2:
            source = jnp.where(inner_ref[0] != 0, source, sources[2 + core][...])
        rows_out = picked(chosen_ref[...], terms(source))
        for turn in range(chips):
            outs[turn][core * capacity : (core + 1) * capacity, :] = rows_out[
                turn * capacity : (turn + 1) * capacity
            ]


def pick(inner, asked, number, sources, chips, capacity):
    rows, width = sources[0].shape
    block = jax.ShapeDtypeStruct((2 * capacity, width), jnp.float32)
    return pl.pallas_call(
        functools.partial(pick_kernel, chips, capacity, number),
        in_specs=[SMEM] + [VMEM] * (len(asked) + len(sources)),
        out_specs=[VMEM] * chips,
        out_shape=[block] * chips,
        scratch_shapes=[pltpu.VMEM((chips * capacity, rows), jnp.bfloat16)],
        cost_estimate=cost(HINT * 12 * chips * capacity * rows * width, 5 * rows * width),
        compiler_params=LIMIT,
        name="pick",
    )(inner, *asked, *sources)


def store_terms(blocks, terms_ref):
    start = 0
    for block in blocks:
        for number, part in enumerate(terms(block[...])):
            terms_ref[number, start : start + block.shape[0], :] = part
        start += block.shape[0]


def placed(place, terms_ref):
    count = terms_ref.shape[1]
    lane = lax.broadcasted_iota(jnp.int32, place.shape, 1)
    chosen = [jnp.where(place - start == lane, 1.0, 0.0) for start in range(0, count, 128)]
    chosen = jnp.concatenate(chosen, axis=1).astype(jnp.bfloat16)
    return picked(chosen, [terms_ref[number] for number in range(3)])


def place_kernel(number, place_ref, *refs):
    blocks, out_ref, terms_ref = refs[:-2], refs[-2], refs[-1]
    store_terms(blocks, terms_ref)
    out_ref[...] = placed(place_ref[number], terms_ref)


def place(number, places, blocks):
    rows = places.shape[1]
    width = blocks[0].shape[1]
    total = sum(block.shape[0] for block in blocks)
    return pl.pallas_call(
        functools.partial(place_kernel, number),
        in_specs=[VMEM] * (1 + len(blocks)),
        out_specs=VMEM,
        out_shape=jax.ShapeDtypeStruct((rows, width), jnp.float32),
        scratch_shapes=[pltpu.VMEM((3, total, width), jnp.bfloat16)],
        cost_estimate=cost(HINT * 3 * 2 * total * rows * width, 3 * rows * width),
        compiler_params=LIMIT,
        name="place",
    )(places, *blocks)


def on_tile(values, at, change):
    parts = [values[:, :at], change(values[:, at : at + 128]), values[:, at + 128 :]]
    return jnp.concatenate([part for part in parts if part.shape[1]], axis=1)


def cleared(lane):
    return lambda tile: jnp.where(lax.broadcasted_iota(jnp.int32, tile.shape, 1) == lane, 0.0, tile)


def before_of(values):
    return on_tile(pltpu.roll(values, 1, 1), 0, cleared(0))


def after_of(values):
    columns = values.shape[1]
    return on_tile(pltpu.roll(values, columns - 1, 1), columns - 128, cleared(127))


def taylor(coeffs, counted):
    before, after = before_of(coeffs), after_of(coeffs)
    bend = after - 2.0 * coeffs + before
    return counted(coeffs + bend * (1.0 / 6.0)), counted(0.5 * (after - before)), counted(bend)


def lanes(values):
    rows, columns = values.shape
    total = values[:, 0:128]
    for start in range(128, columns, 128):
        total = total + values[:, start : start + 128]
    sums = [jnp.sum(total[start : start + 128].T, axis=0, keepdims=True) for start in range(0, rows, 128)]
    return jnp.concatenate(sums, axis=1)


def row_sums(sign, stream, voxels, counted):
    value, slope, bend = taylor(stream, counted)
    value = value - counted(voxels)
    slope = sign * slope
    c0 = slope * slope
    return (
        lanes(slope * value),
        lanes(c0 + bend * value),
        lanes(c0),
        lanes(2.0 * (slope * bend)),
        lanes(bend * bend),
    )


STEP = 128


def all_but_last(values):
    return on_tile(values, values.shape[1] - 128, cleared(127))


def near_sums_kernel(sign_ref, table_ref, near_ref, vol_ref, start_ref, class_ref, out_ref):
    rows, half = near_ref.shape
    for start in range(0, rows, STEP):
        at = slice(start, start + STEP)
        lines = row_sums(sign_ref[0], near_ref[at], vol_ref[at, :half], all_but_last)
        for number, line in enumerate(lines):
            out_ref[number : number + 1, at] = line
    weight = jnp.zeros(start_ref.shape, jnp.float32)
    for kind in range(table_ref.shape[0]):
        weight = jnp.where(class_ref[...] == kind, table_ref[kind], weight)
    out_ref[5:6, :] = start_ref[...]
    out_ref[6:7, :] = jnp.sqrt(weight)
    out_ref[7:8, :] = jnp.zeros(start_ref.shape, jnp.float32)


def near_sums(sign, table, near, voxels, start, classes):
    rows, half = near.shape
    return pl.pallas_call(
        near_sums_kernel,
        in_specs=[SMEM, SMEM] + [VMEM] * 4,
        out_specs=VMEM,
        out_shape=jax.ShapeDtypeStruct((FIELDS, rows), jnp.float32),
        cost_estimate=cost(HINT * 5000 * rows * half, 5 * rows * half),
        compiler_params=LIMIT,
        name="near_sums",
    )(sign, table, near, voxels, start, classes)


def only_last(values):
    lane = lax.broadcasted_iota(jnp.int32, (values.shape[0], 128), 1)
    return on_tile(values, 0, lambda tile: jnp.where(lane == 127, tile, 0.0))


def far_sums_kernel(inner_ref, sign_ref, near_ref, far_ref, hop_ref, vol_ref, so_far_ref, out_ref):
    rows, half = far_ref.shape
    inner = inner_ref[0] != 0
    sign = sign_ref[0]
    for start in range(0, rows, STEP):
        at = slice(start, start + STEP)
        near, far, voxels = near_ref[at], far_ref[at], vol_ref[at, :half]
        lines = row_sums(-sign, far, voxels, all_but_last)
        wide = jnp.concatenate([near[:, half - 128 :], hop_ref[at]], axis=1)
        others = row_sums(sign, wide, vol_ref[at, half - 128 :], only_last)
        for number, (line, other) in enumerate(zip(lines, others)):
            line = line + jnp.where(inner, other, 0.0)
            out_ref[number : number + 1, at] = so_far_ref[number : number + 1, at] + line
    out_ref[5:8, :] = so_far_ref[5:8, :]


def far_sums(inner, sign, near, far, hop, voxels, so_far):
    rows, half = far.shape
    return pl.pallas_call(
        far_sums_kernel,
        in_specs=[SMEM, SMEM] + [VMEM] * 5,
        out_specs=VMEM,
        out_shape=jax.ShapeDtypeStruct((FIELDS, rows), jnp.float32),
        cost_estimate=cost(60 * rows * half, 5 * rows * half),
        compiler_params=LIMIT,
        name="far_sums",
    )(inner, sign, near, far, hop, voxels, so_far)


def right_sums_kernel(inner_ref, sign_ref, place_ref, near_ref, far_ref, vol_ref, so_far_ref, *refs):
    blocks, fields_ref, third_ref, terms_ref = refs[:-3], refs[-3], refs[-2], refs[-1]
    rows, half = near_ref.shape
    inner = inner_ref[0] != 0
    sign = jnp.where(inner, -sign_ref[0], sign_ref[0])
    store_terms(blocks, terms_ref)
    third_ref[...] = placed(place_ref[2], terms_ref)
    for start in range(0, rows, STEP):
        at = slice(start, start + STEP)
        rim = jnp.where(inner, far_ref[at, half - 128 :], near_ref[at, half - 128 :])
        stream = jnp.concatenate([rim, third_ref[at]], axis=1)
        for number, line in enumerate(row_sums(sign, stream, vol_ref[at, half - 128 :], only_last)):
            fields_ref[number : number + 1, at] = so_far_ref[number : number + 1, at] + line
    fields_ref[5:8, :] = so_far_ref[5:8, :]


def right_sums(inner, sign, places, near, far, voxels, so_far, blocks):
    rows, half = near.shape
    total = sum(block.shape[0] for block in blocks)
    return pl.pallas_call(
        right_sums_kernel,
        in_specs=[SMEM, SMEM] + [VMEM] * (5 + len(blocks)),
        out_specs=[VMEM, VMEM],
        out_shape=[
            jax.ShapeDtypeStruct((FIELDS, rows), jnp.float32),
            jax.ShapeDtypeStruct((rows, half), jnp.float32),
        ],
        scratch_shapes=[pltpu.VMEM((3, total, half), jnp.bfloat16)],
        cost_estimate=cost(3 * 2 * total * rows * half, 5 * rows * half),
        compiler_params=LIMIT,
        name="right_sums",
    )(inner, sign, places, near, far, voxels, so_far, *blocks)


def plane_stencil(field):
    slabs, rows = field.shape
    hops = Y // rows
    slab = lax.broadcasted_iota(jnp.int32, field.shape, 0)
    row = lax.broadcasted_iota(jnp.int32, field.shape, 1)

    def moved(cells, by):
        kept = slab >= by if by > 0 else slab < slabs + by
        return jnp.where(kept, pltpu.roll(cells, by % slabs, 0), 0.0)

    low = pltpu.roll(field, 1, 1)
    high = pltpu.roll(field, rows - 1, 1)
    low = jnp.where(row == 0, moved(low, 1), low)
    high = jnp.where(row == rows - 1, moved(high, -1), high)
    return 4.0 * field - low - high - moved(field, hops) - moved(field, -hops)


def total(parts):
    return jnp.sum(functools.reduce(jnp.add, parts), keepdims=True)


def iterate(groups):
    velocities = [group[5] for group in groups]
    for _ in range(ITERS):
        uppers, lowers, directions = [], [], []
        for (l0, l1, c0, c1, c2, _, stiffness, _), velocity in zip(groups, velocities):
            linear = l0 + velocity * (l1 + velocity * (0.75 * c1 + velocity * (0.5 * c2)))
            curvature = c0 + velocity * (c1 + velocity * c2)
            gradient = linear + stiffness * plane_stencil(stiffness * velocity)
            direction = gradient / (curvature + 4.0 * stiffness * stiffness)
            scaled = stiffness * direction
            uppers.append(direction * gradient)
            lowers.append(curvature * direction * direction + scaled * plane_stencil(scaled))
            directions.append(direction)
        alpha = total(uppers) / total(lowers)
        velocities = [velocity - alpha * direction for velocity, direction in zip(velocities, directions)]
    return velocities[0]


def shape_kernel(inner_ref, sign_ref, near_ref, far_ref, hop_ref, third_ref, vol_ref, flat_ref, tilt_ref, curl_ref):
    inner = inner_ref[0] != 0
    for start in range(0, near_ref.shape[0], STEP):
        at = slice(start, start + STEP)
        third = third_ref[at]
        near = jnp.concatenate([near_ref[at], jnp.where(inner, hop_ref[at], third)], axis=1)
        far = jnp.concatenate([far_ref[at], jnp.where(inner, third, 0.0)], axis=1)
        both, drift = near + far, (0.5 * sign_ref[0]) * (near - far)
        bend = after_of(both) - 2.0 * both + before_of(both)
        flat_ref[at] = both + bend * (1.0 / 6.0) - 2.0 * vol_ref[at]
        tilt_ref[at] = after_of(drift) - before_of(drift)
        curl_ref[at] = 0.5 * bend


def shapes(inner, sign, streams, voxels):
    rows, columns = voxels.shape
    return pl.pallas_call(
        shape_kernel,
        in_specs=[SMEM, SMEM] + [VMEM] * 5,
        out_specs=[VMEM] * 3,
        out_shape=[jax.ShapeDtypeStruct((rows, columns), jnp.float32)] * 3,
        cost_estimate=cost(30 * rows * columns, 7 * rows * columns),
        compiler_params=LIMIT,
        name="shapes",
    )(inner, sign, *streams, voxels)


def final_kernel(chips, at_ref, *refs):
    fields_refs = refs[:-8]
    flat_ref, tilt_ref, curl_ref, velocity_ref, misfit_ref, fields_ref, tile_ref, sent = refs[-8:]
    rows, columns = flat_ref.shape
    if chips:
        scans = len(fields_refs) // 2
        for number, ref in enumerate(fields_refs):
            core = (at_ref[0] + number // scans) % 2
            for turn in range(chips):
                slab = 2 * ((at_ref[0] // 2 - turn + chips) % chips) + core
                fields_ref[number % scans, slab] = ref[FIELDS * turn : FIELDS * turn + FIELDS, :]
        groups = [[fields_ref[scan, :, i, :] for i in range(FIELDS)] for scan in range(scans)]
    else:
        groups = [[ref[:, i, :] for i in range(FIELDS)] for ref in fields_refs]
    velocity = iterate(groups)
    slab = lax.broadcasted_iota(jnp.int32, velocity.shape, 0)
    own = jnp.sum(jnp.where(slab == at_ref[0], velocity, 0.0), axis=0, keepdims=True)
    velocity_ref[...] = own

    copies = []
    for number, start in enumerate(range(0, rows, STEP)):
        at = slice(start, start + STEP)
        moved = jnp.concatenate([column(own[:, at])] * (columns // 128), axis=1)
        tile_ref[number] = flat_ref[at] + moved * (tilt_ref[at] + moved * curl_ref[at])
        copies.append(pltpu.make_async_copy(tile_ref.at[number], misfit_ref.at[pl.ds(start, STEP)], sent.at[number]))
        copies[-1].start()
    for copy in copies:
        copy.wait()


def finish(at, groups, parts, chips):
    rows, columns = parts[0].shape
    steps = rows // STEP
    shape = (len(groups) // 2, 2 * chips, FIELDS, rows) if chips else (1, 1, 8, 128)
    return pl.pallas_call(
        functools.partial(final_kernel, chips),
        in_specs=[SMEM] + [VMEM] * (len(groups) + 3),
        out_specs=[VMEM, pl.BlockSpec(memory_space=pl.ANY)],
        out_shape=[
            jax.ShapeDtypeStruct((1, rows), jnp.float32),
            jax.ShapeDtypeStruct((rows, columns), jnp.float32),
        ],
        scratch_shapes=[
            pltpu.VMEM(shape, jnp.float32),
            pltpu.VMEM((steps, STEP, columns), jnp.float32),
            pltpu.SemaphoreType.DMA((steps,)),
        ],
        compiler_params=LIMIT,
        name="finish",
    )(at, *groups, *parts)


def swapped(block, axis):
    return lax.all_to_all(block, axis, split_axis=0, concat_axis=0, tiled=True)


def after(block, *earlier):
    return lax.optimization_barrier((block, *earlier))[0]


def on_device(volume, velocity0, fetch_slab, fetch_row, modulus_class, modulus_table):
    voxels = volume[0]
    rows = voxels.shape[0]
    slabs = lax.axis_size("slab")
    scans = lax.axis_size("scan")
    capacity = max(2, 3 * rows // (2 * slabs))
    direct = slabs == 8
    scan = lax.axis_index("scan")
    slab = lax.axis_index("slab")
    at = slab.astype(jnp.int32).reshape(1)
    inner = ((scan == 1) | (scan == 2)).astype(jnp.int32).reshape(1)
    sign = jnp.where(scan % 2 == 0, 1.0, -1.0).astype(jnp.float32).reshape(1)
    sides = [(0, 1), (1, 0), (2, 3), (3, 2)]
    middle = [(1, 2), (2, 1)]

    names = fetch_slab[0, :, :, 0] * rows + fetch_row[0]
    lent = jnp.where(scan % 2 == 0, names[0:1], names[1:2])
    own = jnp.where(scan < 2, names[0:1], names[1:2])
    side, inward = lax.ppermute(lent, "scan", sides), lax.ppermute(own, "scan", middle)
    places, tables = requests(inner, at, side, inward, own, slabs, capacity, direct)
    chips = slabs // 2
    turns = [[(p, (p + 2 * turn) % slabs) for p in range(slabs)] for turn in range(chips)]
    if direct:
        asked = tables[:1] + [lax.ppermute(tables[turn], "slab", turns[turn]) for turn in range(1, chips)]
    else:
        asked = [swapped(tables[0], "slab")]

    def other_core(block):
        return lax.ppermute(block, "slab", [(p, p ^ 1) for p in range(slabs)]) if direct else block

    left, right = prefilter(voxels, names)
    left, right, _ = lax.optimization_barrier((left, right, tables[0]))
    left_other, right_other = other_core(left), other_core(right)
    from_inner = lax.ppermute(right, "scan", [(1, 0), (2, 3)])
    from_middle = lax.ppermute(right, "scan", middle)

    def picks(number, sources):
        if direct:
            return pick(inner, asked, number, sources, chips, capacity)
        source = sources[0] if len(sources) == 2 else jnp.where(inner[0] != 0, sources[0], sources[2])
        wanted = asked[0][:, 128 * number : 128 * number + capacity]
        return [jnp.take(source, wanted.reshape(-1), axis=0)]

    sent = []

    def fetched(blocks, order, before_last=()):
        if not direct:
            arrived = swapped(blocks[0].reshape(slabs, capacity, -1), "slab")
            return [arrived.reshape(slabs * capacity, -1)]
        arrived = [blocks[0]] + [None] * (chips - 1)
        for turn in order:
            held = sent[-3:-2] + (list(before_last) if turn == order[-1] else [])
            block = after(blocks[turn], *held) if held else blocks[turn]
            arrived[turn] = lax.ppermute(block, "slab", turns[turn])
            sent.append(arrived[turn])
        return arrived

    arrived = fetched(picks(0, [left, left_other]), (3, 1, 2))
    first = place(0, places, arrived)
    lender = jnp.where(inner == 1, after(from_middle, *arrived), from_inner)
    near = lax.ppermute(first, "scan", sides)
    arrived2 = fetched(picks(1, [left, left_other, right, right_other]), (3, 1, 2))
    blocks = picks(2, [lender, other_core(lender)])
    second = place(1, places, [after(arrived2[0], blocks[0]), *arrived2[1:]])
    arrived = fetched(blocks, (3, 1, 2))
    hop = lax.ppermute(second, "scan", [(0, 1), (3, 2)])
    far = lax.ppermute(second, "scan", middle)
    begun = arrived[3:4] if direct else arrived
    so_far = near_sums(sign, modulus_table, after(near, *begun), voxels, velocity0, modulus_class)
    so_far = far_sums(inner, sign, near, far, hop, voxels, so_far)
    sums, third = right_sums(inner, sign, places, near, far, voxels, so_far, arrived)

    def scans_of(block):
        routes = [[(p, (p + turn) % scans) for p in range(scans)] for turn in range(1, scans)]
        return [block] + [lax.ppermute(block, "scan", route) for route in routes]

    parts = shapes(inner, sign, (near, far, hop, third), voxels)
    if direct:
        line = jnp.concatenate([sums] + [lax.ppermute(sums, "slab", route) for route in turns[1:]], axis=0)
        line = after(line, parts[0])
        groups = scans_of(line)
        groups += [other_core(group) for group in groups]
    else:
        groups = scans_of(swapped(jnp.broadcast_to(sums[None], (slabs, FIELDS, rows)), "slab"))
    velocity, misfit = finish(at, groups, parts, chips if direct else 0)
    return velocity, misfit[None]


def solution(mesh):
    return jax.shard_map(
        on_device,
        mesh=mesh,
        in_specs=(
            P("scan", "slab", None),
            P("scan", "slab"),
            P("scan", None, "slab", None),
            P("scan", None, "slab"),
            P("scan", "slab"),
            P(),
        ),
        out_specs=(P("scan", "slab"), P("scan", "slab", None)),
        check_vma=False,
    )
```

```python
import functools
import math

import jax
import jax.numpy as jnp
from jax import lax
from jax.experimental import pallas as pl
from jax.experimental.pallas import tpu as pltpu
from jax.sharding import PartitionSpec as P

Y = 1024
BAND = 32
ITERS = 2
FIELDS = 8
HINT = 16
VMEM = pl.BlockSpec(memory_space=pltpu.VMEM)
SMEM = pl.BlockSpec(memory_space=pltpu.SMEM)
LIMIT = pltpu.CompilerParams(vmem_limit_bytes=20 * 1024 * 1024)


def cost(flops, values):
    return pl.CostEstimate(flops=flops, bytes_accessed=4 * values, transcendentals=0)


def store_filter(rim, high_ref, low_ref):
    shape = high_ref.shape
    distance = jnp.abs(lax.broadcasted_iota(jnp.int32, shape, 0) - rim - lax.broadcasted_iota(jnp.int32, shape, 1))
    parity = 1.0 - 2.0 * (distance % 2).astype(jnp.float32)
    size = jnp.exp(distance.astype(jnp.float32) * math.log(2.0 - math.sqrt(3.0)))
    exact = jnp.where(distance <= BAND, math.sqrt(3.0) * parity * size, 0.0)
    high = exact.astype(jnp.bfloat16)
    high_ref[...] = high
    low_ref[...] = (exact - high.astype(jnp.float32)).astype(jnp.bfloat16)


def prefilter_kernel(width, rim, vol_ref, early_ref, left_ref, right_ref, high_ref, low_ref, held_ref, sent):
    rows, columns = vol_ref.shape
    half = columns // 2
    steps = held_ref.shape[0]
    block = rows // steps
    copies = [
        pltpu.make_async_copy(vol_ref.at[pl.ds(number * block, block)], held_ref.at[number], sent.at[number])
        for number in range(steps)
    ]
    for copy in copies:
        copy.start()
    store_filter(rim, high_ref, low_ref)
    for number, copy in enumerate(copies):
        copy.wait()
        at = slice(number * block, (number + 1) * block)
        voxels = held_ref[number]
        high = voxels.astype(jnp.bfloat16)
        low = (voxels - high.astype(jnp.float32)).astype(jnp.bfloat16)
        for start in range(0, columns, width):
            first, last = max(0, start - rim), min(columns, start + width + rim)
            top = first - (start - rim)
            band = slice(top, top + last - first)
            dot = functools.partial(jnp.dot, preferred_element_type=jnp.float32)
            out = dot(high[:, first:last], low_ref[band, :]) + dot(low[:, first:last], high_ref[band, :])
            out = out + dot(high[:, first:last], high_ref[band, :])
            if start < half:
                left_ref[at, start : start + width] = out
            else:
                right_ref[at, start - half : start - half + width] = out


def prefilter(voxels, early):
    rows, columns = voxels.shape
    width, rim, steps = 256, 128, 2
    halves = jax.ShapeDtypeStruct((rows, columns // 2), jnp.float32)
    matrix = pltpu.VMEM((width + 2 * rim, width), jnp.bfloat16)
    anywhere = pl.BlockSpec(memory_space=pl.ANY)
    return pl.pallas_call(
        functools.partial(prefilter_kernel, width, rim),
        in_specs=[pl.BlockSpec(memory_space=pltpu.HBM), anywhere],
        out_specs=[VMEM, VMEM],
        out_shape=[halves, halves],
        scratch_shapes=[
            matrix,
            matrix,
            pltpu.VMEM((steps, rows // steps, columns), jnp.float32),
            pltpu.SemaphoreType.DMA((steps,)),
        ],
        cost_estimate=cost(3 * 2 * rows * columns * (width + 2 * rim), 2 * rows * columns),
        compiler_params=LIMIT,
        name="prefilter",
    )(voxels, early)


def column(line):
    parts = [
        jnp.broadcast_to(line[:, start : start + 128], (128, 128)).T for start in range(0, line.shape[1], 128)
    ]
    return parts[0] if len(parts) == 1 else jnp.concatenate(parts, axis=0)


def request_kernel(devices, capacity, direct, inner_ref, at_ref, side_ref, inward_ref, own_ref, place_ref, *table_refs):
    rows = own_ref.shape[1]
    before = lax.broadcasted_iota(jnp.int32, (rows, rows), 0)
    after = lax.broadcasted_iota(jnp.int32, (rows, rows), 1)
    earlier = jnp.where(before < after, 1.0, 0.0).astype(jnp.bfloat16)
    peers = lax.broadcasted_iota(jnp.int32, (devices, rows), 0)
    chip, core, chips = at_ref[0] // 2, at_ref[0] % 2, devices // 2
    slots = lax.broadcasted_iota(jnp.int32, (128, rows), 0)
    against = (((1,), (1,)), ((), ()))
    side = side_ref[...]
    for number, name in enumerate((side, jnp.where(inner_ref[0] != 0, inward_ref[...], side), own_ref[...])):
        peer = name // rows
        row = name - peer * rows
        turn = peer
        if direct:
            other = (peer + core) % 2
            turn = 2 * ((chip - peer // 2 + chips) % chips) + other
            peer = 2 * ((peer // 2 - chip + chips) % chips) + other
        hit = jnp.where(peers == peer, 1.0, 0.0)
        running = jnp.dot(hit.astype(jnp.bfloat16), earlier, preferred_element_type=jnp.float32)
        slot = jnp.sum(hit * running, axis=0, keepdims=True).astype(jnp.int32)
        place_ref[number] = column(turn * capacity + slot)
        taken = jnp.where(slots == slot, 1.0, 0.0).astype(jnp.bfloat16)
        upper = (hit * (row // 16).astype(jnp.float32)).astype(jnp.bfloat16)
        lower = (hit * (row % 16).astype(jnp.float32)).astype(jnp.bfloat16)
        found = 16.0 * lax.dot_general(upper, taken, against, preferred_element_type=jnp.float32)
        found = found + lax.dot_general(lower, taken, against, preferred_element_type=jnp.float32)
        share = devices // len(table_refs)
        for turn, table_ref in enumerate(table_refs):
            lines = found[turn * share : (turn + 1) * share].astype(jnp.int32)
            table_ref[:, 128 * number : 128 * number + 128] = lines


def requests(inner, at, side, inward, own, devices, capacity, direct):
    rows = own.shape[1]
    parts = devices // 2 if direct else 1
    places, *tables = pl.pallas_call(
        functools.partial(request_kernel, devices, capacity, direct),
        in_specs=[SMEM, SMEM, VMEM, VMEM, VMEM],
        out_specs=[VMEM] * (1 + parts),
        out_shape=[jax.ShapeDtypeStruct((3, rows, 128), jnp.int32)]
        + [jax.ShapeDtypeStruct((devices // parts, 3 * 128), jnp.int32)] * parts,
        compiler_params=LIMIT,
        name="requests",
    )(inner, at, side, inward, own)
    return places, tables


def terms(values):
    high = values.astype(jnp.bfloat16)
    rest = values - high.astype(jnp.float32)
    middle = rest.astype(jnp.bfloat16)
    low = (rest - middle.astype(jnp.float32)).astype(jnp.bfloat16)
    return high, middle, low


def picked(chosen, parts):
    dot = functools.partial(jnp.dot, preferred_element_type=jnp.float32)
    return (dot(chosen, parts[2]) + dot(chosen, parts[1])) + dot(chosen, parts[0])


def pick_kernel(chips, capacity, number, inner_ref, *refs):
    asked_refs, refs = refs[:chips], refs[chips:]
    sources, outs, chosen_ref = refs[: -1 - chips], refs[-1 - chips : -1], refs[-1]
    rows = sources[0].shape[0]
    row = lax.broadcasted_iota(jnp.int32, (128, rows), 1)
    for core in range(2):
        for turn in range(chips):
            back = (chips - turn) % chips
            line = asked_refs[back][core : core + 1, 128 * number : 128 * number + 128]
            wanted = jnp.concatenate([column(line)] * (rows // 128), axis=1)
            hit = jnp.where(wanted == row, 1.0, 0.0)[:capacity]
            chosen_ref[turn * capacity : (turn + 1) * capacity, :] = hit.astype(jnp.bfloat16)
        source = sources[core][...]
        if len(sources) > 2:
            source = jnp.where(inner_ref[0] != 0, source, sources[2 + core][...])
        rows_out = picked(chosen_ref[...], terms(source))
        for turn in range(chips):
            outs[turn][core * capacity : (core + 1) * capacity, :] = rows_out[
                turn * capacity : (turn + 1) * capacity
            ]


def pick(inner, asked, number, sources, chips, capacity):
    rows, width = sources[0].shape
    block = jax.ShapeDtypeStruct((2 * capacity, width), jnp.float32)
    return pl.pallas_call(
        functools.partial(pick_kernel, chips, capacity, number),
        in_specs=[SMEM] + [VMEM] * (len(asked) + len(sources)),
        out_specs=[VMEM] * chips,
        out_shape=[block] * chips,
        scratch_shapes=[pltpu.VMEM((chips * capacity, rows), jnp.bfloat16)],
        cost_estimate=cost(HINT * 12 * chips * capacity * rows * width, 5 * rows * width),
        compiler_params=LIMIT,
        name="pick",
    )(inner, *asked, *sources)


def store_terms(blocks, terms_ref):
    start = 0
    for block in blocks:
        for number, part in enumerate(terms(block[...])):
            terms_ref[number, start : start + block.shape[0], :] = part
        start += block.shape[0]


def placed(place, terms_ref):
    count = terms_ref.shape[1]
    lane = lax.broadcasted_iota(jnp.int32, place.shape, 1)
    chosen = [jnp.where(place - start == lane, 1.0, 0.0) for start in range(0, count, 128)]
    chosen = jnp.concatenate(chosen, axis=1).astype(jnp.bfloat16)
    return picked(chosen, [terms_ref[number] for number in range(3)])


def place_kernel(number, place_ref, *refs):
    blocks, out_ref, terms_ref = refs[:-2], refs[-2], refs[-1]
    store_terms(blocks, terms_ref)
    out_ref[...] = placed(place_ref[number], terms_ref)


def place(number, places, blocks):
    rows = places.shape[1]
    width = blocks[0].shape[1]
    total = sum(block.shape[0] for block in blocks)
    return pl.pallas_call(
        functools.partial(place_kernel, number),
        in_specs=[VMEM] * (1 + len(blocks)),
        out_specs=VMEM,
        out_shape=jax.ShapeDtypeStruct((rows, width), jnp.float32),
        scratch_shapes=[pltpu.VMEM((3, total, width), jnp.bfloat16)],
        cost_estimate=cost(HINT * 3 * 2 * total * rows * width, 3 * rows * width),
        compiler_params=LIMIT,
        name="place",
    )(places, *blocks)


def on_tile(values, at, change):
    parts = [values[:, :at], change(values[:, at : at + 128]), values[:, at + 128 :]]
    return jnp.concatenate([part for part in parts if part.shape[1]], axis=1)


def cleared(lane):
    return lambda tile: jnp.where(lax.broadcasted_iota(jnp.int32, tile.shape, 1) == lane, 0.0, tile)


def before_of(values):
    return on_tile(pltpu.roll(values, 1, 1), 0, cleared(0))


def after_of(values):
    columns = values.shape[1]
    return on_tile(pltpu.roll(values, columns - 1, 1), columns - 128, cleared(127))


def taylor(coeffs, counted):
    before, after = before_of(coeffs), after_of(coeffs)
    bend = after - 2.0 * coeffs + before
    return counted(coeffs + bend * (1.0 / 6.0)), counted(0.5 * (after - before)), counted(bend)


def lanes(values):
    rows, columns = values.shape
    total = values[:, 0:128]
    for start in range(128, columns, 128):
        total = total + values[:, start : start + 128]
    sums = [jnp.sum(total[start : start + 128].T, axis=0, keepdims=True) for start in range(0, rows, 128)]
    return jnp.concatenate(sums, axis=1)


def row_sums(sign, stream, voxels, counted):
    value, slope, bend = taylor(stream, counted)
    value = value - counted(voxels)
    slope = sign * slope
    c0 = slope * slope
    return (
        lanes(slope * value),
        lanes(c0 + bend * value),
        lanes(c0),
        lanes(2.0 * (slope * bend)),
        lanes(bend * bend),
    )


STEP = 128


def all_but_last(values):
    return on_tile(values, values.shape[1] - 128, cleared(127))


def near_sums_kernel(sign_ref, table_ref, near_ref, vol_ref, start_ref, class_ref, out_ref):
    rows, half = near_ref.shape
    for start in range(0, rows, STEP):
        at = slice(start, start + STEP)
        lines = row_sums(sign_ref[0], near_ref[at], vol_ref[at, :half], all_but_last)
        for number, line in enumerate(lines):
            out_ref[number : number + 1, at] = line
    weight = jnp.zeros(start_ref.shape, jnp.float32)
    for kind in range(table_ref.shape[0]):
        weight = jnp.where(class_ref[...] == kind, table_ref[kind], weight)
    out_ref[5:6, :] = start_ref[...]
    out_ref[6:7, :] = jnp.sqrt(weight)
    out_ref[7:8, :] = jnp.zeros(start_ref.shape, jnp.float32)


def near_sums(sign, table, near, voxels, start, classes):
    rows, half = near.shape
    return pl.pallas_call(
        near_sums_kernel,
        in_specs=[SMEM, SMEM] + [VMEM] * 4,
        out_specs=VMEM,
        out_shape=jax.ShapeDtypeStruct((FIELDS, rows), jnp.float32),
        cost_estimate=cost(HINT * 5000 * rows * half, 5 * rows * half),
        compiler_params=LIMIT,
        name="near_sums",
    )(sign, table, near, voxels, start, classes)


def only_last(values):
    lane = lax.broadcasted_iota(jnp.int32, (values.shape[0], 128), 1)
    return on_tile(values, 0, lambda tile: jnp.where(lane == 127, tile, 0.0))


def far_sums_kernel(inner_ref, sign_ref, near_ref, far_ref, hop_ref, vol_ref, so_far_ref, out_ref):
    rows, half = far_ref.shape
    inner = inner_ref[0] != 0
    sign = sign_ref[0]
    for start in range(0, rows, STEP):
        at = slice(start, start + STEP)
        near, far, voxels = near_ref[at], far_ref[at], vol_ref[at, :half]
        lines = row_sums(-sign, far, voxels, all_but_last)
        wide = jnp.concatenate([near[:, half - 128 :], hop_ref[at]], axis=1)
        others = row_sums(sign, wide, vol_ref[at, half - 128 :], only_last)
        for number, (line, other) in enumerate(zip(lines, others)):
            line = line + jnp.where(inner, other, 0.0)
            out_ref[number : number + 1, at] = so_far_ref[number : number + 1, at] + line
    out_ref[5:8, :] = so_far_ref[5:8, :]


def far_sums(inner, sign, near, far, hop, voxels, so_far):
    rows, half = far.shape
    return pl.pallas_call(
        far_sums_kernel,
        in_specs=[SMEM, SMEM] + [VMEM] * 5,
        out_specs=VMEM,
        out_shape=jax.ShapeDtypeStruct((FIELDS, rows), jnp.float32),
        cost_estimate=cost(60 * rows * half, 5 * rows * half),
        compiler_params=LIMIT,
        name="far_sums",
    )(inner, sign, near, far, hop, voxels, so_far)


def right_sums_kernel(inner_ref, sign_ref, place_ref, near_ref, far_ref, vol_ref, so_far_ref, *refs):
    blocks, fields_ref, third_ref, terms_ref = refs[:-3], refs[-3], refs[-2], refs[-1]
    rows, half = near_ref.shape
    inner = inner_ref[0] != 0
    sign = jnp.where(inner, -sign_ref[0], sign_ref[0])
    store_terms(blocks, terms_ref)
    third_ref[...] = placed(place_ref[2], terms_ref)
    for start in range(0, rows, STEP):
        at = slice(start, start + STEP)
        rim = jnp.where(inner, far_ref[at, half - 128 :], near_ref[at, half - 128 :])
        stream = jnp.concatenate([rim, third_ref[at]], axis=1)
        for number, line in enumerate(row_sums(sign, stream, vol_ref[at, half - 128 :], only_last)):
            fields_ref[number : number + 1, at] = so_far_ref[number : number + 1, at] + line
    fields_ref[5:8, :] = so_far_ref[5:8, :]


def right_sums(inner, sign, places, near, far, voxels, so_far, blocks):
    rows, half = near.shape
    total = sum(block.shape[0] for block in blocks)
    return pl.pallas_call(
        right_sums_kernel,
        in_specs=[SMEM, SMEM] + [VMEM] * (5 + len(blocks)),
        out_specs=[VMEM, VMEM],
        out_shape=[
            jax.ShapeDtypeStruct((FIELDS, rows), jnp.float32),
            jax.ShapeDtypeStruct((rows, half), jnp.float32),
        ],
        scratch_shapes=[pltpu.VMEM((3, total, half), jnp.bfloat16)],
        cost_estimate=cost(3 * 2 * total * rows * half, 5 * rows * half),
        compiler_params=LIMIT,
        name="right_sums",
    )(inner, sign, places, near, far, voxels, so_far, *blocks)


def plane_stencil(field):
    slabs, rows = field.shape
    hops = Y // rows
    slab = lax.broadcasted_iota(jnp.int32, field.shape, 0)
    row = lax.broadcasted_iota(jnp.int32, field.shape, 1)

    def moved(cells, by):
        kept = slab >= by if by > 0 else slab < slabs + by
        return jnp.where(kept, pltpu.roll(cells, by % slabs, 0), 0.0)

    low = pltpu.roll(field, 1, 1)
    high = pltpu.roll(field, rows - 1, 1)
    low = jnp.where(row == 0, moved(low, 1), low)
    high = jnp.where(row == rows - 1, moved(high, -1), high)
    return 4.0 * field - low - high - moved(field, hops) - moved(field, -hops)


def total(parts):
    return jnp.sum(functools.reduce(jnp.add, parts), keepdims=True)


def iterate(groups):
    velocities = [group[5] for group in groups]
    for _ in range(ITERS):
        uppers, lowers, directions = [], [], []
        for (l0, l1, c0, c1, c2, _, stiffness, _), velocity in zip(groups, velocities):
            linear = l0 + velocity * (l1 + velocity * (0.75 * c1 + velocity * (0.5 * c2)))
            curvature = c0 + velocity * (c1 + velocity * c2)
            gradient = linear + stiffness * plane_stencil(stiffness * velocity)
            direction = gradient / (curvature + 4.0 * stiffness * stiffness)
            scaled = stiffness * direction
            uppers.append(direction * gradient)
            lowers.append(curvature * direction * direction + scaled * plane_stencil(scaled))
            directions.append(direction)
        alpha = total(uppers) / total(lowers)
        velocities = [velocity - alpha * direction for velocity, direction in zip(velocities, directions)]
    return velocities[0]


def shape_kernel(inner_ref, sign_ref, near_ref, far_ref, hop_ref, third_ref, vol_ref, flat_ref, tilt_ref, curl_ref):
    inner = inner_ref[0] != 0
    for start in range(0, near_ref.shape[0], STEP):
        at = slice(start, start + STEP)
        third = third_ref[at]
        near = jnp.concatenate([near_ref[at], jnp.where(inner, hop_ref[at], third)], axis=1)
        far = jnp.concatenate([far_ref[at], jnp.where(inner, third, 0.0)], axis=1)
        both, drift = near + far, (0.5 * sign_ref[0]) * (near - far)
        bend = after_of(both) - 2.0 * both + before_of(both)
        flat_ref[at] = both + bend * (1.0 / 6.0) - 2.0 * vol_ref[at]
        tilt_ref[at] = after_of(drift) - before_of(drift)
        curl_ref[at] = 0.5 * bend


def shapes(inner, sign, streams, voxels):
    rows, columns = voxels.shape
    return pl.pallas_call(
        shape_kernel,
        in_specs=[SMEM, SMEM] + [VMEM] * 5,
        out_specs=[VMEM] * 3,
        out_shape=[jax.ShapeDtypeStruct((rows, columns), jnp.float32)] * 3,
        cost_estimate=cost(30 * rows * columns, 7 * rows * columns),
        compiler_params=LIMIT,
        name="shapes",
    )(inner, sign, *streams, voxels)


def final_kernel(chips, at_ref, *refs):
    fields_refs = refs[:-8]
    flat_ref, tilt_ref, curl_ref, velocity_ref, misfit_ref, fields_ref, tile_ref, sent = refs[-8:]
    rows, columns = flat_ref.shape
    if chips:
        scans = len(fields_refs) // 2
        for number, ref in enumerate(fields_refs):
            core = (at_ref[0] + number // scans) % 2
            for turn in range(chips):
                slab = 2 * ((at_ref[0] // 2 - turn + chips) % chips) + core
                fields_ref[number % scans, slab] = ref[FIELDS * turn : FIELDS * turn + FIELDS, :]
        groups = [[fields_ref[scan, :, i, :] for i in range(FIELDS)] for scan in range(scans)]
    else:
        groups = [[ref[:, i, :] for i in range(FIELDS)] for ref in fields_refs]
    velocity = iterate(groups)
    slab = lax.broadcasted_iota(jnp.int32, velocity.shape, 0)
    own = jnp.sum(jnp.where(slab == at_ref[0], velocity, 0.0), axis=0, keepdims=True)
    velocity_ref[...] = own

    copies = []
    for number, start in enumerate(range(0, rows, STEP)):
        at = slice(start, start + STEP)
        moved = jnp.concatenate([column(own[:, at])] * (columns // 128), axis=1)
        tile_ref[number] = flat_ref[at] + moved * (tilt_ref[at] + moved * curl_ref[at])
        copies.append(pltpu.make_async_copy(tile_ref.at[number], misfit_ref.at[pl.ds(start, STEP)], sent.at[number]))
        copies[-1].start()
    for copy in copies:
        copy.wait()


def finish(at, groups, parts, chips):
    rows, columns = parts[0].shape
    steps = rows // STEP
    shape = (len(groups) // 2, 2 * chips, FIELDS, rows) if chips else (1, 1, 8, 128)
    return pl.pallas_call(
        functools.partial(final_kernel, chips),
        in_specs=[SMEM] + [VMEM] * (len(groups) + 3),
        out_specs=[VMEM, pl.BlockSpec(memory_space=pl.ANY)],
        out_shape=[
            jax.ShapeDtypeStruct((1, rows), jnp.float32),
            jax.ShapeDtypeStruct((rows, columns), jnp.float32),
        ],
        scratch_shapes=[
            pltpu.VMEM(shape, jnp.float32),
            pltpu.VMEM((steps, STEP, columns), jnp.float32),
            pltpu.SemaphoreType.DMA((steps,)),
        ],
        compiler_params=LIMIT,
        name="finish",
    )(at, *groups, *parts)


def swapped(block, axis):
    return lax.all_to_all(block, axis, split_axis=0, concat_axis=0, tiled=True)


def after(block, *earlier):
    return lax.optimization_barrier((block, *earlier))[0]


def on_device(volume, velocity0, fetch_slab, fetch_row, modulus_class, modulus_table):
    voxels = volume[0]
    rows = voxels.shape[0]
    slabs = lax.axis_size("slab")
    scans = lax.axis_size("scan")
    capacity = max(2, 3 * rows // (2 * slabs))
    direct = slabs == 8
    scan = lax.axis_index("scan")
    slab = lax.axis_index("slab")
    at = slab.astype(jnp.int32).reshape(1)
    inner = ((scan == 1) | (scan == 2)).astype(jnp.int32).reshape(1)
    sign = jnp.where(scan % 2 == 0, 1.0, -1.0).astype(jnp.float32).reshape(1)
    sides = [(0, 1), (1, 0), (2, 3), (3, 2)]
    middle = [(1, 2), (2, 1)]

    names = fetch_slab[0, :, :, 0] * rows + fetch_row[0]
    lent = jnp.where(scan % 2 == 0, names[0:1], names[1:2])
    own = jnp.where(scan < 2, names[0:1], names[1:2])
    side, inward = lax.ppermute(lent, "scan", sides), lax.ppermute(own, "scan", middle)
    places, tables = requests(inner, at, side, inward, own, slabs, capacity, direct)
    chips = slabs // 2
    turns = [[(p, (p + 2 * turn) % slabs) for p in range(slabs)] for turn in range(chips)]
    if direct:
        asked = tables[:1] + [lax.ppermute(tables[turn], "slab", turns[turn]) for turn in range(1, chips)]
    else:
        asked = [swapped(tables[0], "slab")]

    def other_core(block):
        return lax.ppermute(block, "slab", [(p, p ^ 1) for p in range(slabs)]) if direct else block

    left, right = prefilter(voxels, names)
    left, right, _ = lax.optimization_barrier((left, right, tables[0]))
    left_other, right_other = other_core(left), other_core(right)
    from_inner = lax.ppermute(right, "scan", [(1, 0), (2, 3)])
    from_middle = lax.ppermute(right, "scan", middle)

    def picks(number, sources):
        if direct:
            return pick(inner, asked, number, sources, chips, capacity)
        source = sources[0] if len(sources) == 2 else jnp.where(inner[0] != 0, sources[0], sources[2])
        wanted = asked[0][:, 128 * number : 128 * number + capacity]
        return [jnp.take(source, wanted.reshape(-1), axis=0)]

    sent = []

    def fetched(blocks, order, before_last=()):
        if not direct:
            arrived = swapped(blocks[0].reshape(slabs, capacity, -1), "slab")
            return [arrived.reshape(slabs * capacity, -1)]
        arrived = [blocks[0]] + [None] * (chips - 1)
        for turn in order:
            held = sent[-3:-2] + (list(before_last) if turn == order[-1] else [])
            block = after(blocks[turn], *held) if held else blocks[turn]
            arrived[turn] = lax.ppermute(block, "slab", turns[turn])
            sent.append(arrived[turn])
        return arrived

    arrived = fetched(picks(0, [left, left_other]), (3, 1, 2))
    first = place(0, places, arrived)
    lender = jnp.where(inner == 1, after(from_middle, *arrived[1::2]), from_inner)
    near = lax.ppermute(first, "scan", sides)
    arrived2 = fetched(picks(1, [left, left_other, right, right_other]), (3, 1, 2))
    blocks = picks(2, [lender, other_core(lender)])
    second = place(1, places, [after(arrived2[0], blocks[0]), *arrived2[1:]])
    arrived = fetched(blocks, (3, 1, 2))
    far = lax.ppermute(second, "scan", middle)
    hop = lax.ppermute(second, "scan", [(0, 1), (3, 2)])
    begun = arrived[3:4] if direct else arrived
    so_far = near_sums(sign, modulus_table, after(near, *begun), voxels, velocity0, modulus_class)
    so_far = far_sums(inner, sign, near, far, hop, voxels, so_far)
    sums, third = right_sums(inner, sign, places, near, far, voxels, so_far, arrived)

    def scans_of(block):
        routes = [[(p, (p + turn) % scans) for p in range(scans)] for turn in range(1, scans)]
        return [block] + [lax.ppermute(block, "scan", route) for route in routes]

    parts = shapes(inner, sign, (near, far, hop, third), voxels)
    if direct:
        line = jnp.concatenate([sums] + [lax.ppermute(sums, "slab", route) for route in turns[1:]], axis=0)
        line = after(line, parts[0])
        groups = scans_of(line)
        groups += [other_core(group) for group in groups]
    else:
        groups = scans_of(swapped(jnp.broadcast_to(sums[None], (slabs, FIELDS, rows)), "slab"))
    velocity, misfit = finish(at, groups, parts, chips if direct else 0)
    return velocity, misfit[None]


def solution(mesh):
    return jax.shard_map(
        on_device,
        mesh=mesh,
        in_specs=(
            P("scan", "slab", None),
            P("scan", "slab"),
            P("scan", None, "slab", None),
            P("scan", None, "slab"),
            P("scan", "slab"),
            P(),
        ),
        out_specs=(P("scan", "slab"), P("scan", "slab", None)),
        check_vma=False,
    )
```
